256 devices in a mesh: sec: 2 (over core), tm: 32 (over z, y), dp: 4 (over x).
Axes of the slice: x: 4, y: 4, z: 8, core: 2. Of those that a mesh axis runs over, the one named last changes fastest.
Arguments:
- enc_input: bfloat16 [4, 32768, 1024], P('dp', ('sec', 'tm')), may hold values from -6 to 6
- llm_grads: bfloat16 [4, 65536, 1024], P('dp', ('sec', 'tm')), may hold values from -6 to 6
- slot_block: int32 [4, 4096], P('dp', ('sec', 'tm')), may hold values from -1 to 2047, as said below
- utt_lengths: int32 [4, 262], P('dp'), may hold values from 1 to 250, 32768 in all within a row
- ln_gain: float32 [1024], replicated, may hold values from 0.1 to 1.9
- ln_bias: float32 [1024], replicated, may hold values from -3 to 3
- w_in: bfloat16 [1024, 2048], replicated, may hold values from -0.1875 to 0.1875
- dw_kernel: float32 [9, 1024], replicated, may hold values from -2 to 2
- bn_gain: float32 [1024], replicated, may hold values from 0.1 to 1.9
- bn_bias: float32 [1024], replicated, may hold values from -3 to 3
- w_out: bfloat16 [1024, 1024], replicated, may hold values from -0.1875 to 0.1875
Outputs:
- grad_input: bfloat16 [4, 32768, 1024], P('dp', ('sec', 'tm'))
The draws below stay inside these ranges and needn't reach their ends.
Inputs may be any that keep to these rules, and one draw needn't show every extreme that they name: `slot_block`: in each group every block 0 to 2047 stands in exactly one slot and the other slots hold -1; block b holds the timeline frames b * 16 to b * 16 + 15. The 64 slots of one device hold at most 1 block of any one timeline device, and for every timeline device some device's slots hold exactly 1 of its blocks. `utt_lengths`: each group's lengths sum to 32768, and the largest is 250.
All inputs are finite; a program needn't handle non-finite values.
Results may differ from the reference program's by a relative error of at most 0.0048.
Values may be sent and summed in bfloat16 or wider, within the bound.
A program may use at most 64 MiB of HBM per device.

```python
import math
import jax
import jax.numpy as jnp
import numpy as np
from jax import lax

C = 1024
KER = 9
FR_DEV = 512
NBE = 32
MAXLEN = 250
SHARDS = 64
GROUPS = 4
BLK = 16
NS = 64
CAPB = 1
UTT = 262


def draw_slot_block(key, part):
    key = jax.random.fold_in(key, 11)
    tokens = jnp.repeat(jnp.arange(SHARDS, dtype=jnp.int32), CAPB)

    def one_receiver(recv_key):
        key_a, key_b, key_c = jax.random.split(recv_key, 3)
        forced = jax.random.randint(key_a, (), 0, SHARDS)
        scores = jax.random.permutation(key_b, 2 * NBE).astype(jnp.int32)
        scores = jnp.where(tokens == forced, -1 - jnp.arange(2 * NBE, dtype=jnp.int32), scores)
        order_idx = jnp.argsort(scores)
        senders = tokens[order_idx[:NBE]]
        return senders[jax.random.permutation(key_c, NBE)]

    def one_group(group_key):
        key_a, key_b = jax.random.split(group_key, 2)
        senders = jax.vmap(one_receiver)(jax.random.split(key_a, SHARDS))
        flat_senders = senders.reshape(-1)
        onehot = (flat_senders[:, None] == jnp.arange(SHARDS, dtype=jnp.int32)[None, :]).astype(jnp.int32)
        rank_in = jnp.sum((jnp.cumsum(onehot, axis=0) - onehot) * onehot, axis=1)
        slot_perm = jax.vmap(lambda slot_key: jax.random.permutation(slot_key, NS).astype(jnp.int32))(jax.random.split(key_b, SHARDS))
        slot_pos = flat_senders * NS + slot_perm[flat_senders, rank_in]
        result = jnp.full((SHARDS * NS,), -1, jnp.int32)
        return result.at[slot_pos].set(jnp.arange(SHARDS * NBE, dtype=jnp.int32))
    return jax.vmap(one_group)(jax.random.split(key, GROUPS))


def draw_llm_grads(key, part):
    key = jax.random.fold_in(key, 5)
    key_a, key_b = jax.random.split(key, 2)
    shape_all = (GROUPS, SHARDS * NS * BLK, C)
    channel_shift = jax.random.uniform(key_b, (GROUPS, 1, C), jnp.float32, -1.2, 1.2)
    base_vals = jnp.clip(jax.random.normal(key_a, shape_all, jnp.float32), -4.0, 4.0)
    return (base_vals + channel_shift).astype(jnp.bfloat16)


def draw_enc_input(key, part):
    key = jax.random.fold_in(key, 7)
    key_a, key_b, key_c = jax.random.split(key, 3)
    eighth = SHARDS * FR_DEV // 8
    half_pattern = 0.6 * jnp.clip(jax.random.normal(key_b, (GROUPS, 2, 1, 1, C), jnp.float32), -2.5, 2.5)
    part_pattern = 0.4 * jnp.clip(jax.random.normal(key_c, (GROUPS, 2, 4, 1, C), jnp.float32), -2.5, 2.5)
    shape_all = (GROUPS, 2, 4, eighth, C)
    base_vals = jnp.clip(jax.random.normal(key_a, shape_all, jnp.float32), -3.5, 3.5)
    values = base_vals + half_pattern + part_pattern
    return values.reshape(GROUPS, SHARDS * FR_DEV, C).astype(jnp.bfloat16)


def length_profile(number_of, total, limit, skew):
    loads = [(1 << 20) // math.isqrt(grade ** skew) + 1 for grade in range(2, number_of + 1)]
    surplus, holding = total - limit - (number_of - 1), [1] * (number_of - 1)
    while surplus > 0:
        candidates = [i for i in range(number_of - 1) if holding[i] < limit]
        mass, remaining = sum([loads[i] for i in candidates]), surplus
        for i in candidates:
            addition = min(limit - holding[i], max(1, remaining * loads[i] // mass), surplus)
            holding[i] = holding[i] + addition
            surplus = surplus - addition
    return np.array([limit] + holding)


def uneven_parts(rng, number_of, total, reach, slope):
    if number_of == 2:
        one = jax.random.randint(rng, (), max(1, total - reach), min(reach, total - 1) + 1)
        return jnp.stack([one, total - one])
    lengths = jnp.asarray(length_profile(number_of, total, reach, slope), jnp.int32)
    twos = (number_of - 1) // 2
    donor, sink = lengths[1:1 + 2 * twos:2], lengths[2:2 + 2 * twos:2]
    margin = jnp.minimum(donor - 1, reach - sink)
    moved = jax.random.randint(jax.random.fold_in(rng, 1), (twos,), 0, 1 << 20) % (margin + 1)
    lengths = lengths.at[1:1 + 2 * twos:2].set(donor - moved).at[2:2 + 2 * twos:2].set(sink + moved)
    return lengths[jax.random.permutation(jax.random.fold_in(rng, 2), number_of)]


def scatter_about(stream_key, shape, spread, limit, held_as=jnp.bfloat16):
    array = spread * jax.random.normal(stream_key, shape, jnp.float32)
    return jnp.clip(array, min=-limit, max=limit).astype(held_as)


def setup_inputs(seed: int = 0) -> dict:
    seeds = jax.random.split(jax.random.key(seed), 12)
    enc_input = draw_enc_input(jax.random.fold_in(seeds[11], 71), 0)
    llm_grads = draw_llm_grads(jax.random.fold_in(seeds[11], 71), 0)
    slot_block = draw_slot_block(jax.random.fold_in(seeds[11], 71), 0)
    utt_lengths = jax.vmap(lambda own: uneven_parts(own, UTT, SHARDS * FR_DEV, MAXLEN, 2))(jax.random.split(seeds[3], GROUPS)).reshape((GROUPS, UTT)).astype(jnp.int32)
    ln_gain = jnp.clip(1.0 + 0.18 * jax.random.normal(seeds[4], (C,), jnp.float32), 0.1, 1.9)
    ln_bias = scatter_about(seeds[5], (C,), 0.5, 3.0, jnp.float32)
    w_in = scatter_about(seeds[6], (C, 2 * C), C ** -0.5, 0.1875)
    dw_kernel = scatter_about(seeds[7], (KER, C), KER ** -0.5, 2.0, jnp.float32)
    bn_gain = jnp.clip(1.0 + 0.18 * jax.random.normal(seeds[8], (C,), jnp.float32), 0.1, 1.9)
    bn_bias = scatter_about(seeds[9], (C,), 0.5, 3.0, jnp.float32)
    w_out = scatter_about(seeds[10], (C, C), C ** -0.5, 0.1875)
    return {"enc_input": enc_input, "llm_grads": llm_grads, "slot_block": slot_block, "utt_lengths": utt_lengths, "ln_gain": ln_gain, "ln_bias": ln_bias, "w_in": w_in, "dw_kernel": dw_kernel, "bn_gain": bn_gain, "bn_bias": bn_bias, "w_out": w_out}


norm_eps = 1e-05

def regroup_rows(grad_rows, slot_ids):
    block_count = SHARDS * NBE
    slot_count = SHARDS * NS
    blocks_in = grad_rows.reshape(slot_count, BLK * C)
    target = jnp.where(slot_ids >= 0, slot_ids, block_count).astype(jnp.int32)
    source = jnp.zeros((block_count + 1,), jnp.int32).at[target].set(jnp.arange(slot_count, dtype=jnp.int32))
    return blocks_in[source[:block_count]].reshape(block_count * BLK, C)

def segment_of(lengths_row):
    timeline = SHARDS * FR_DEV
    utt_ends = jnp.cumsum(lengths_row.astype(jnp.int32)).astype(jnp.int32)
    positions = jnp.arange(timeline, dtype=jnp.int32)
    return lax.optimization_barrier(jnp.sum((positions[:, None] >= utt_ends[None, :]).astype(jnp.int32), axis=1))

def agree_ref(segment, offset):
    timeline = SHARDS * FR_DEV
    moved = jnp.arange(timeline, dtype=jnp.int32) + offset
    inside = (moved >= 0) & (moved < timeline)
    other = segment[jnp.clip(moved, 0, timeline - 1)]
    return (inside & (other == segment)).astype(jnp.float32)[:, None]

def shifted(values, offset, half_width):
    padded = jnp.pad(values, ((half_width, half_width), (0, 0)))
    return padded[half_width + offset:half_width + offset + values.shape[0]]

def reference(enc_input, llm_grads, slot_block, utt_lengths, ln_gain, ln_bias, w_in, dw_kernel, bn_gain, bn_bias, w_out):
    half_width = (KER - 1) // 2
    frame_total = float(GROUPS * SHARDS * FR_DEV)
    stash_one = []
    sum_first = jnp.zeros((C,), jnp.float32)
    sum_second = jnp.zeros((C,), jnp.float32)
    for group_idx in range(GROUPS):
        incoming = regroup_rows(llm_grads[group_idx], slot_block[group_idx])
        x_float = enc_input[group_idx].astype(jnp.float32)
        row_mean = lax.optimization_barrier(jnp.mean(x_float, axis=1, keepdims=True))
        centred = x_float - row_mean
        row_rstd = lax.rsqrt(lax.optimization_barrier(jnp.mean(centred * centred, axis=1, keepdims=True)) + norm_eps)
        x_hat = centred * row_rstd
        normed = (x_hat * ln_gain + ln_bias).astype(jnp.bfloat16)
        mixed_proj = jnp.dot(normed, w_in, preferred_element_type=jnp.float32)
        lin_part = mixed_proj[:, :C]
        gate_part = mixed_proj[:, C:]
        gated_out = (lin_part * jax.nn.sigmoid(gate_part)).astype(jnp.bfloat16)
        segment = segment_of(utt_lengths[group_idx])
        gated_float = gated_out.astype(jnp.float32)
        conv_out = jnp.zeros_like(gated_float)
        for tap_idx in range(KER):
            offset = tap_idx - half_width
            conv_out = conv_out + dw_kernel[tap_idx] * agree_ref(segment, offset) * shifted(gated_float, offset, half_width)
        sum_first = sum_first + lax.optimization_barrier(jnp.sum(conv_out, axis=0))
        sum_second = sum_second + lax.optimization_barrier(jnp.sum(conv_out * conv_out, axis=0))
        stash_one.append((incoming, x_hat, row_rstd, lin_part, gate_part, segment, conv_out))
    bn_mean = sum_first / frame_total
    bn_var = sum_second / frame_total - bn_mean * bn_mean
    bn_rstd = lax.rsqrt(bn_var + norm_eps)
    stash_two = []
    sum_grad = jnp.zeros((C,), jnp.float32)
    sum_cross = jnp.zeros((C,), jnp.float32)
    for group_idx in range(GROUPS):
        incoming, x_hat, row_rstd, lin_part, gate_part, segment, conv_out = stash_one[group_idx]
        z_hat = (conv_out - bn_mean) * bn_rstd
        pre_act = z_hat * bn_gain + bn_bias
        sig_pre = jax.nn.sigmoid(pre_act)
        back_swish = jnp.dot(incoming, w_out.T, preferred_element_type=jnp.float32)
        d_pre = back_swish * sig_pre * (1.0 + pre_act * (1.0 - sig_pre))
        sum_grad = sum_grad + lax.optimization_barrier(jnp.sum(d_pre, axis=0))
        sum_cross = sum_cross + lax.optimization_barrier(jnp.sum(d_pre * z_hat, axis=0))
        stash_two.append((z_hat, d_pre))
    grad_mean = sum_grad / frame_total
    cross_mean = sum_cross / frame_total
    results = []
    for group_idx in range(GROUPS):
        incoming, x_hat, row_rstd, lin_part, gate_part, segment, conv_out = stash_one[group_idx]
        z_hat, d_pre = stash_two[group_idx]
        d_conv = (bn_gain * bn_rstd * (d_pre - grad_mean - z_hat * cross_mean)).astype(jnp.bfloat16)
        conv_float = d_conv.astype(jnp.float32)
        d_gated = jnp.zeros_like(conv_float)
        for tap_idx in range(KER):
            offset = half_width - tap_idx
            d_gated = d_gated + dw_kernel[tap_idx] * agree_ref(segment, offset) * shifted(conv_float, offset, half_width)
        gate_sig = jax.nn.sigmoid(gate_part)
        d_mixed = jnp.concatenate([d_gated * gate_sig, d_gated * lin_part * gate_sig * (1.0 - gate_sig)], axis=1).astype(jnp.bfloat16)
        d_normed = jnp.dot(d_mixed, w_in.T, preferred_element_type=jnp.float32)
        h_term = d_normed * ln_gain
        back_norm = row_rstd * (h_term - lax.optimization_barrier(jnp.mean(h_term, axis=1, keepdims=True)) - x_hat * lax.optimization_barrier(jnp.mean(h_term * x_hat, axis=1, keepdims=True)))
        results.append((incoming.astype(jnp.float32) + back_norm).astype(jnp.bfloat16))
    return jnp.stack(results)
```

```python
import functools

import jax
import jax.numpy as jnp
from jax import lax
from jax.experimental import pallas as pl
from jax.experimental.pallas import tpu as pltpu
from jax.sharding import PartitionSpec as P

MESH = pl.DeviceIdType.MESH
F32 = jnp.float32
BF16 = jnp.bfloat16
I32 = jnp.int32

EPS = 1e-05
SEC, NZ, NY, NX = 2, 8, 4, 4
SHARDS = SEC * NZ * NY
FRAMES = 512
C = 1024
TAPS = 9
HALF = 4
PAD = 8
EXT = FRAMES + 2 * PAD
BLK = 16
NBE = 32
UTT = 262
UTT_PAD = 384
LANES = 128
COLS = C // LANES
ROWS = 128
WIN = 6
SENDS = SHARDS - 1
ALL_FRAMES = float(FRAMES * SHARDS * NX)
NT = (((1,), (1,)), ((), ()))


def wrap(value, count):
    return lax.rem(value + count, count)


def kernel(
    enc_hbm,
    llm_hbm,
    w_in_hbm,
    w_out_hbm,
    slot_ref,
    utt_ref,
    ln_gain_ref,
    ln_bias_ref,
    dw_ref,
    bn_gain_ref,
    bn_bias_ref,
    out_hbm,
    enc,
    llm,
    w_in,
    w_out,
    send,
    recv,
    row_buf,
    slot_tbl,
    src_tbl,
    ids_line,
    ids_tile,
    ids_all,
    utt_pad,
    seg,
    masks,
    x_hat,
    rstd,
    normed,
    sig,
    dsig,
    gated,
    conv,
    swish,
    ones_t,
    z_t,
    d_t,
    d_pre,
    inc,
    d_mixed,
    h_buf,
    out_buf,
    ar_src,
    ar_s,
    ar_xy,
    ar_z,
    load_sem,
    tbl_sem,
    a2a_send,
    a2a_recv,
    ids_send,
    ids_recv,
    halo_send,
    halo_recv,
    ar_send,
    ar_recv,
    out_sem,
):
    sec = lax.axis_index("sec")
    tm = lax.axis_index("tm")
    dp = lax.axis_index("dp")
    z = tm // NY
    y = lax.rem(tm, NY)
    me = sec * (NZ * NY) + tm

    def place(s_at, z_at, y_at, x_at):
        return {"sec": s_at, "tm": z_at * NY + y_at, "dp": x_at}

    loads = []
    for k, (source, target) in enumerate(
        ((llm_hbm, llm), (enc_hbm, enc), (w_in_hbm, w_in), (w_out_hbm, w_out))
    ):
        load = pltpu.make_async_copy(source, target, load_sem.at[k])
        load.start()
        loads.append(load)

    def partner(i):
        k = lax.rem(i, NZ)
        q = 7 - i // NZ
        dz = 4 + ((k + 1) // 2) * (1 - 2 * lax.rem(k, 2))
        return (
            lax.rem(sec + lax.rem(q, 2), SEC),
            lax.rem(z + dz, NZ),
            lax.rem(y + q // 2, NY),
        )

    line = [(sec, wrap(z + d, NZ), y, dp) for d in (4, 3, 5, 2, 6, 1, 7)]
    cross = [
        (sec, z, wrap(y + j, NY), wrap(dp + i, NX))
        for j in (2, 1, 3, 0)
        for i in (2, 1, 3, 0)
        if (i, j) != (0, 0)
    ]
    mate = [(1 - sec, z, y, dp)]
    plane = [
        (wrap(sec + s, SEC), z, wrap(y + j, NY), dp)
        for j in (2, 1, 3, 0)
        for s in (1, 0)
        if (s, j) != (0, 0)
    ]

    barrier = pltpu.get_barrier_semaphore()

    def greet(i, carry):
        s_at, z_at, y_at = partner(i)
        pl.semaphore_signal(
            barrier, inc=1, device_id=place(s_at, z_at, y_at, dp), device_id_type=MESH
        )
        return carry

    lax.fori_loop(0, SENDS, greet, 0)
    others = [p for p, keep in zip(cross, [i != 0 for j in (2, 1, 3, 0) for i in (2, 1, 3, 0) if (i, j) != (0, 0)]) if keep]
    for p in others:
        pl.semaphore_signal(barrier, inc=1, device_id=place(*p), device_id_type=MESH)

    slot_row = slot_ref[...]
    lane = lax.broadcasted_iota(I32, (64, LANES), 1)
    sub = lax.broadcasted_iota(I32, (64, LANES), 0)
    lane64 = lax.broadcasted_iota(I32, (64, 64), 1)
    sub64 = lax.broadcasted_iota(I32, (64, 64), 0)
    slot_col = jnp.sum(
        jnp.where(lane64 == sub64, jnp.broadcast_to(slot_row, (64, 64)), 0), axis=1, keepdims=True
    )
    hit = (slot_col >= lane * NBE) & (slot_col < lane * NBE + NBE)
    row_buf[0:1, :] = jnp.sum(jnp.where(hit, sub, 0), axis=0, keepdims=True)
    ids_row = jnp.sum(jnp.where(hit, slot_col + 1, 0), axis=0, keepdims=True) - 1
    tbl = pltpu.make_async_copy(row_buf.at[pl.ds(0, 1)], slot_tbl, tbl_sem.at[0])
    tbl.start()
    ids_line[z] = ids_row
    loads[0].wait()
    tbl.wait()

    def pack(d, carry):
        send[d] = llm[jnp.clip(slot_tbl[0, d], 0, 63)]
        return carry

    lax.fori_loop(0, SHARDS, pack, 0)
    recv[me] = send[me]

    pl.semaphore_wait(barrier, SENDS + len(others))

    def spread(partners, source, target_of, s_sem, r_sem):
        for i, p in enumerate(partners):
            pltpu.make_async_remote_copy(
                source, target_of(i), s_sem, r_sem, device_id=place(*p), device_id_type=MESH
            ).start()

    def wait_bytes(ref, sem):
        pltpu.make_async_copy(ref, ref, sem).wait()

    spread(line, ids_line.at[z], lambda i: ids_line.at[z], ids_send.at[0], ids_recv.at[0])

    def block_copy(i):
        s_at, z_at, y_at = partner(i)
        to = s_at * (NZ * NY) + z_at * NY + y_at
        return pltpu.make_async_remote_copy(
            send.at[to],
            recv.at[me],
            a2a_send.at[lax.rem(i, WIN)],
            a2a_recv,
            device_id=place(s_at, z_at, y_at, dp),
            device_id_type=MESH,
        )

    def first(i, carry):
        block_copy(i).start()
        return carry

    lax.fori_loop(0, WIN, first, 0)
    sent = [WIN]

    def pump_one(i):
        block_copy(i - WIN).wait_send()
        block_copy(i).start()

    def pump(count):
        low = sent[0]
        high = min(SENDS, low + count)
        sent[0] = high
        if high > low:

            def step(i, carry):
                pump_one(i)
                return carry

            lax.fori_loop(low, high, step, 0)

    def pumped(count):
        low = sent[0]
        assert low + count <= SENDS
        sent[0] = low + count
        return low

    loads[1].wait()
    gain = ln_gain_ref[...]
    bias = ln_bias_ref[...]

    def norm(r, carry):
        rows = pl.ds(pl.multiple_of(r * 64, 64), 64)
        values = enc[rows, :].astype(F32)
        mean = jnp.mean(values, axis=1, keepdims=True)
        centred = values - mean
        scale = lax.rsqrt(jnp.mean(centred * centred, axis=1, keepdims=True) + EPS)
        hat = centred * scale
        rstd[rows, :] = jnp.broadcast_to(scale, (64, LANES))
        x_hat[rows, :] = hat
        normed[rows, :] = (hat * gain + bias).astype(BF16)
        return carry

    lax.fori_loop(0, 8, norm, 0)
    pump(2)

    loads[2].wait()
    low = pumped(8)

    def project(n, carry):
        at = pl.ds(pl.multiple_of(n * 256, 256), 256)
        gate_at = pl.ds(pl.multiple_of(C + n * 256, 256), 256)
        lin = jnp.dot(normed[...], w_in[:, at], preferred_element_type=F32)
        gate = jnp.dot(normed[...], w_in[:, gate_at], preferred_element_type=F32)
        pump_one(low + 2 * n)
        s = jax.nn.sigmoid(gate)
        mixed = lin * s
        sig[:, at] = s
        dsig[:, at] = mixed * (1.0 - s)
        gated[pl.ds(PAD, FRAMES), at] = mixed.astype(BF16).astype(F32)
        pump_one(low + 2 * n + 1)
        return carry

    lax.fori_loop(0, 4, project, 0)

    before = wrap(me + SHARDS - 1, SHARDS)
    after = wrap(me + 1, SHARDS)

    def edges(buf, k):
        for j, (to, start, end) in enumerate(
            ((after, FRAMES, 0), (before, PAD, PAD + FRAMES))
        ):
            pltpu.make_async_remote_copy(
                buf.at[pl.ds(start, PAD)],
                buf.at[pl.ds(end, PAD)],
                halo_send.at[k, j],
                halo_recv.at[k, j],
                device_id={"sec": to // (NZ * NY), "tm": lax.rem(to, NZ * NY), "dp": dp},
                device_id_type=MESH,
            ).start()

    def edges_in(buf, k):
        wait_bytes(buf.at[pl.ds(0, PAD)], halo_recv.at[k, 0])
        wait_bytes(buf.at[pl.ds(PAD + FRAMES, PAD)], halo_recv.at[k, 1])

    def edges_out(buf, k):
        wait_bytes(buf.at[pl.ds(0, PAD)], halo_send.at[k, 0])
        wait_bytes(buf.at[pl.ds(0, PAD)], halo_send.at[k, 1])

    edges(gated, 0)

    wait_bytes(ids_line.at[pl.ds(0, NZ - 1)], ids_recv.at[0])
    for j in range(NZ):
        ids_tile[j : j + 1, :] = ids_line[j]
    here = sec * NY + y
    ids_all[here] = ids_tile[...]
    spread(plane, ids_tile, lambda i: ids_all.at[here], ids_send.at[1], ids_recv.at[1])

    utt_pad[...] = jnp.zeros((8, UTT_PAD), I32)
    utt_pad[0:1, 0:UTT] = utt_ref[...]
    lengths = utt_pad[...].astype(F32).astype(BF16)
    upper = (
        lax.broadcasted_iota(I32, (UTT_PAD, UTT_PAD), 0)
        <= lax.broadcasted_iota(I32, (UTT_PAD, UTT_PAD), 1)
    ).astype(F32).astype(BF16)
    ends = jnp.dot(lengths, upper, preferred_element_type=F32)[0:1, :]

    def number(r, carry):
        rows = pl.ds(pl.multiple_of(r * 48, 8), 48)
        position = lax.broadcasted_iota(I32, (48, 1), 0) + (r * 48 + me * FRAMES - PAD)
        position_f = position.astype(F32)
        count = jnp.sum((position_f >= ends).astype(F32), axis=1, keepdims=True)
        inside = (position >= 0) & (position < SHARDS * FRAMES)
        seg[rows, :] = jnp.broadcast_to(jnp.where(inside, count, -1.0), (48, LANES))
        return carry

    lax.fori_loop(0, EXT // 48, number, 0)

    def mark(r, carry):
        window = seg[pl.ds(pl.multiple_of(r * ROWS, ROWS), ROWS + 2 * PAD), :]
        own = window[PAD : PAD + ROWS]
        rows = pl.ds(pl.multiple_of(r * ROWS, ROWS), ROWS)
        for j in range(TAPS):
            masks[j, rows, :] = (window[HALF + j : HALF + j + ROWS] == own).astype(F32)
        return carry

    lax.fori_loop(0, FRAMES // ROWS, mark, 0)
    pump(5)
    edges_in(gated, 0)

    low_conv = pumped(8)

    def convolve(c, carry):
        cols = pl.ds(pl.multiple_of(c * LANES, LANES), LANES)
        taps = dw_ref[:, cols]
        first_sum = jnp.zeros((1, LANES), F32)
        second_sum = jnp.zeros((1, LANES), F32)
        for r in range(FRAMES // ROWS):
            window = gated[r * ROWS : r * ROWS + ROWS + 2 * PAD, cols]
            total = jnp.zeros((ROWS, LANES), F32)
            for k in range(TAPS):
                part = window[HALF + k : HALF + k + ROWS]
                if k != HALF:
                    part = part * masks[k, r * ROWS : r * ROWS + ROWS, :]
                total = total + taps[k : k + 1, :] * part
            conv[PAD + r * ROWS : PAD + r * ROWS + ROWS, cols] = total
            first_sum = first_sum + jnp.sum(total, axis=0, keepdims=True)
            second_sum = second_sum + jnp.sum(total * total, axis=0, keepdims=True)
        ar_src[0, 0, 0, pl.ds(c, 1), :] = first_sum
        ar_src[0, 0, 1, pl.ds(c, 1), :] = second_sum
        pump_one(low_conv + c)
        return carry

    lax.fori_loop(0, COLS, convolve, 0)
    edges(conv, 1)

    groups = ((mate, ar_s), (cross, ar_xy), (line, ar_z))

    def sum_send(k, step):
        partners, target = groups[step]
        spread(
            partners,
            ar_src.at[k, step],
            lambda i: target.at[k, i],
            ar_send.at[k, step],
            ar_recv.at[k, step],
        )

    def sum_recv(k, step):
        partners, target = groups[step]
        count = len(partners)
        wait_bytes(target.at[k, pl.ds(0, count)], ar_recv.at[k, step])
        total = ar_src[k, step]
        for i in range(count):
            total = total + target[k, i]
        ar_src[k, step + 1] = total

    def sum_done(k):
        for step, (partners, target) in enumerate(groups):
            wait_bytes(target.at[k, pl.ds(0, len(partners))], ar_send.at[k, step])

    for step, count in ((0, 1), (1, 7), (2, 7)):
        sum_send(0, step)
        pump(count)
        sum_recv(0, step)

    wait_bytes(ids_all.at[pl.ds(0, 7)], ids_recv.at[1])
    ids = ids_all[...].reshape(64, LANES)
    mine = jnp.sum(jnp.where(lane == me, ids, 0), axis=1, keepdims=True) - me * NBE
    quarter = sub // NZ
    source = (quarter // NY) * (NZ * NY) + lax.rem(sub, NZ) * NY + lax.rem(quarter, NY)
    row_buf[1:2, :] = jnp.sum(jnp.where(mine == lane, source, 0), axis=0, keepdims=True)
    src_copy = pltpu.make_async_copy(row_buf.at[pl.ds(1, 1)], src_tbl, tbl_sem.at[1])
    src_copy.start()

    edges_in(conv, 1)
    edges_out(conv, 1)

    low_bn = pumped(8)

    def bn_scales(c):
        bn_mean = ar_src[0, 3, 0, pl.ds(c, 1), :] / ALL_FRAMES
        bn_var = ar_src[0, 3, 1, pl.ds(c, 1), :] / ALL_FRAMES - bn_mean * bn_mean
        return bn_mean, lax.rsqrt(bn_var + EPS)

    def transposed(source, c, r, window_of):
        taps = dw_ref[:, pl.ds(pl.multiple_of(c * LANES, LANES), LANES)]
        return taps

    def normalise(c, carry):
        cols = pl.ds(pl.multiple_of(c * LANES, LANES), LANES)
        bn_mean, bn_rstd = bn_scales(c)
        bn_gain = bn_gain_ref[pl.ds(c, 1), :]
        bn_bias = bn_bias_ref[pl.ds(c, 1), :]
        taps = dw_ref[:, cols]
        factor = bn_gain * bn_rstd
        for r in range(EXT // 48):
            rows = slice(r * 48, r * 48 + 48)
            conv[rows, cols] = (conv[rows, cols] - bn_mean) * bn_rstd
        for r in range(FRAMES // ROWS):
            rows = slice(r * ROWS, r * ROWS + ROWS)
            window = conv[r * ROWS : r * ROWS + ROWS + 2 * PAD, cols]
            pre = window[PAD : PAD + ROWS] * bn_gain + bn_bias
            s = jax.nn.sigmoid(pre)
            swish[rows, cols] = s * (1.0 + pre * (1.0 - s))
            ones_total = jnp.zeros((ROWS, LANES), F32)
            z_total = jnp.zeros((ROWS, LANES), F32)
            for j in range(TAPS):
                weight = (taps[TAPS - 1 - j : TAPS - j, :] * factor) * masks[j, rows, :]
                ones_total = ones_total + weight
                z_total = z_total + weight * window[HALF + j : HALF + j + ROWS]
            ones_t[rows, cols] = ones_total
            z_t[rows, cols] = z_total
        pump_one(low_bn + c)
        return carry

    lax.fori_loop(0, COLS, normalise, 0)
    src_copy.wait()
    loads[3].wait()
    pump(SENDS)

    wait_bytes(recv.at[pl.ds(0, SENDS)], a2a_recv)

    def gather(b, carry):
        inc[pl.ds(pl.multiple_of(b * BLK, BLK), BLK), :] = recv[jnp.clip(src_tbl[0, b], 0, 63)]
        return carry

    lax.fori_loop(0, NBE, gather, 0)

    def back(n, carry):
        at = pl.ds(pl.multiple_of(n * 256, 256), 256)
        grad = lax.dot_general(inc[...], w_out[at, :], NT, preferred_element_type=F32)
        grad = grad * swish[:, at]
        d_pre[pl.ds(PAD, FRAMES), at] = grad
        first_sum = jnp.sum(grad, axis=0, keepdims=True)
        cross_sum = jnp.sum(grad * conv[pl.ds(PAD, FRAMES), at], axis=0, keepdims=True)
        for j in range(2):
            ar_src[1, 0, 0, pl.ds(2 * n + j, 1), :] = first_sum[:, j * LANES : (j + 1) * LANES]
            ar_src[1, 0, 1, pl.ds(2 * n + j, 1), :] = cross_sum[:, j * LANES : (j + 1) * LANES]
        return carry

    lax.fori_loop(0, 4, back, 0)

    def conv_back(c, carry):
        cols = pl.ds(pl.multiple_of(c * LANES, LANES), LANES)
        bn_mean, bn_rstd = bn_scales(c)
        factor = bn_gain_ref[pl.ds(c, 1), :] * bn_rstd
        taps = dw_ref[:, cols] * factor
        for r in range(FRAMES // ROWS):
            rows = slice(r * ROWS, r * ROWS + ROWS)
            window = d_pre[r * ROWS : r * ROWS + ROWS + 2 * PAD, cols]
            total = jnp.zeros((ROWS, LANES), F32)
            for j in range(TAPS):
                part = window[HALF + j : HALF + j + ROWS]
                if j != HALF:
                    part = part * masks[j, rows, :]
                total = total + taps[TAPS - 1 - j : TAPS - j, :] * part
            d_t[rows, cols] = total
        return carry

    sum_send(1, 0)
    edges(d_pre, 2)
    sum_recv(1, 0)
    sum_send(1, 1)
    edges_in(d_pre, 2)
    lax.fori_loop(0, COLS // 2, conv_back, 0)
    sum_recv(1, 1)
    sum_send(1, 2)
    lax.fori_loop(COLS // 2, COLS, conv_back, 0)
    sum_recv(1, 2)

    def assemble(c, carry):
        cols = pl.ds(pl.multiple_of(c * LANES, LANES), LANES)
        gate_cols = pl.ds(pl.multiple_of(C + c * LANES, LANES), LANES)
        grad_mean = ar_src[1, 3, 0, pl.ds(c, 1), :] / ALL_FRAMES
        cross_mean = ar_src[1, 3, 1, pl.ds(c, 1), :] / ALL_FRAMES
        for r in range(FRAMES // ROWS):
            rows = slice(r * ROWS, r * ROWS + ROWS)
            grad = d_t[rows, cols] - grad_mean * ones_t[rows, cols] - cross_mean * z_t[rows, cols]
            d_mixed[rows, cols] = (grad * sig[rows, cols]).astype(BF16)
            d_mixed[rows, gate_cols] = (grad * dsig[rows, cols]).astype(BF16)
        return carry

    lax.fori_loop(0, COLS, assemble, 0)

    def unproject(n, carry):
        at = pl.ds(pl.multiple_of(n * 256, 256), 256)
        grad = lax.dot_general(d_mixed[...], w_in[at, :], NT, preferred_element_type=F32)
        h_buf[:, at] = grad * ln_gain_ref[:, at]
        return carry

    lax.fori_loop(0, 4, unproject, 0)

    stores = []
    for r in range(4):
        rows = pl.ds(r * ROWS, ROWS)

        def finish(k, carry, r=r):
            part = pl.ds(pl.multiple_of(r * ROWS + k * 32, 32), 32)
            h = h_buf[part, :]
            hat = x_hat[part, :]
            mean = jnp.mean(h, axis=1, keepdims=True)
            along = jnp.mean(h * hat, axis=1, keepdims=True)
            scale = rstd[part, 0:1]
            out_buf[part, :] = (inc[part, :].astype(F32) + scale * (h - mean - hat * along)).astype(BF16)
            return carry

        lax.fori_loop(0, 4, finish, 0)
        store = pltpu.make_async_copy(out_buf.at[rows], out_hbm.at[rows], out_sem.at[r])
        store.start()
        stores.append(store)

    def drain(i, carry):
        block_copy(i).wait_send()
        return carry

    lax.fori_loop(SENDS - WIN, SENDS, drain, 0)
    wait_bytes(ids_line.at[pl.ds(0, NZ - 1)], ids_send.at[0])
    wait_bytes(ids_all.at[pl.ds(0, 7)], ids_send.at[1])
    edges_out(gated, 0)
    edges_out(d_pre, 2)
    sum_done(0)
    sum_done(1)
    for store in stores:
        store.wait()


def local(
    enc_input,
    llm_grads,
    slot_block,
    utt_lengths,
    ln_gain,
    ln_bias,
    w_in,
    dw_kernel,
    bn_gain,
    bn_bias,
    w_out,
):
    vmem = pl.BlockSpec(memory_space=pltpu.VMEM)
    hbm = pl.BlockSpec(memory_space=pl.ANY)
    dma = pltpu.SemaphoreType.DMA
    full = pltpu.VMEM((FRAMES, C), F32)
    wide = pltpu.VMEM((EXT, C), F32)
    blocks = pltpu.VMEM((SHARDS, BLK, C), BF16)
    out = pl.pallas_call(
        kernel,
        out_shape=jax.ShapeDtypeStruct((FRAMES, C), BF16),
        in_specs=[hbm] * 4 + [vmem] * 7,
        out_specs=hbm,
        scratch_shapes=[
            pltpu.VMEM((FRAMES, C), BF16),
            blocks,
            pltpu.VMEM((C, 2 * C), BF16),
            pltpu.VMEM((C, C), BF16),
            blocks,
            blocks,
            pltpu.VMEM((8, LANES), I32),
            pltpu.SMEM((1, LANES), I32),
            pltpu.SMEM((1, LANES), I32),
            pltpu.VMEM((NZ, 1, LANES), I32),
            pltpu.VMEM((NZ, LANES), I32),
            pltpu.VMEM((8, NZ, LANES), I32),
            pltpu.VMEM((8, UTT_PAD), I32),
            pltpu.VMEM((EXT, LANES), F32),
            pltpu.VMEM((TAPS, FRAMES, LANES), F32),
            full,
            pltpu.VMEM((FRAMES, LANES), F32),
            pltpu.VMEM((FRAMES, C), BF16),
            full,
            full,
            wide,
            wide,
            full,
            full,
            full,
            full,
            wide,
            pltpu.VMEM((FRAMES, C), BF16),
            pltpu.VMEM((FRAMES, 2 * C), BF16),
            full,
            pltpu.VMEM((FRAMES, C), BF16),
            pltpu.VMEM((2, 4, 2, COLS, LANES), F32),
            pltpu.VMEM((2, 1, 2, COLS, LANES), F32),
            pltpu.VMEM((2, 15, 2, COLS, LANES), F32),
            pltpu.VMEM((2, 7, 2, COLS, LANES), F32),
            dma((4,)),
            dma((2,)),
            dma((WIN,)),
            dma,
            dma((2,)),
            dma((2,)),
            dma((3, 2)),
            dma((3, 2)),
            dma((2, 3)),
            dma((2, 3)),
            dma((4,)),
        ],
        compiler_params=pltpu.CompilerParams(
            collective_id=1, has_side_effects=True, vmem_limit_bytes=56 << 20
        ),
        name="conv_module_back",
    )(
        enc_input[0],
        llm_grads[0].reshape(SHARDS, BLK, C),
        w_in,
        w_out,
        slot_block,
        utt_lengths,
        ln_gain.reshape(1, C),
        ln_bias.reshape(1, C),
        dw_kernel,
        bn_gain.reshape(COLS, LANES),
        bn_bias.reshape(COLS, LANES),
    )
    return out[None]


def solution(mesh):
    in_specs = (
        P("dp", ("sec", "tm"), None),
        P("dp", ("sec", "tm"), None),
        P("dp", ("sec", "tm")),
        P("dp", None),
        P(),
        P(),
        P(),
        P(),
        P(),
        P(),
        P(),
    )
    out_specs = P("dp", ("sec", "tm"), None)
    return jax.shard_map(local, mesh=mesh, in_specs=in_specs, out_specs=out_specs, check_vma=False)
```

```python
import functools

import jax
import jax.numpy as jnp
from jax import lax
from jax.experimental import pallas as pl
from jax.experimental.pallas import tpu as pltpu
from jax.sharding import PartitionSpec as P

MESH = pl.DeviceIdType.MESH
F32 = jnp.float32
BF16 = jnp.bfloat16
I32 = jnp.int32

EPS = 1e-05
SEC, NZ, NY, NX = 2, 8, 4, 4
SHARDS = SEC * NZ * NY
FRAMES = 512
C = 1024
TAPS = 9
HALF = 4
PAD = 8
EXT = FRAMES + 2 * PAD
BLK = 16
NBE = 32
UTT = 262
UTT_PAD = 384
LANES = 128
COLS = C // LANES
ROWS = 128
WIN = 16
SENDS = SHARDS - 1
ALL_FRAMES = float(FRAMES * SHARDS * NX)
NT = (((1,), (1,)), ((), ()))


def wrap(value, count):
    return lax.rem(value + count, count)


def kernel(
    enc_hbm,
    llm_hbm,
    w_in_hbm,
    w_out_hbm,
    slot_ref,
    utt_ref,
    ln_gain_ref,
    ln_bias_ref,
    dw_ref,
    bn_gain_ref,
    bn_bias_ref,
    out_ref,
    enc,
    llm,
    w_in,
    w_out,
    send,
    recv,
    row_buf,
    slot_tbl,
    src_tbl,
    ids_line,
    ids_tile,
    ids_all,
    utt_pad,
    seg,
    masks,
    x_hat,
    rstd,
    normed,
    sig,
    dsig,
    gated,
    conv,
    swish,
    ones_t,
    z_t,
    d_t,
    d_pre,
    inc,
    d_mixed,
    h_buf,
    ar_src,
    ar_s,
    ar_xy,
    ar_z,
    load_sem,
    tbl_sem,
    a2a_send,
    a2a_recv,
    ids_send,
    ids_recv,
    halo_send,
    halo_recv,
    ar_send,
    ar_recv,
    lines_in,
):
    sec = lax.axis_index("sec")
    tm = lax.axis_index("tm")
    dp = lax.axis_index("dp")
    z = tm // NY
    y = lax.rem(tm, NY)
    me = sec * (NZ * NY) + tm

    def place(s_at, z_at, y_at, x_at):
        return {"sec": s_at, "tm": z_at * NY + y_at, "dp": x_at}

    loads = []
    for k, (source, target) in enumerate(
        ((llm_hbm, llm), (enc_hbm, enc), (w_in_hbm, w_in), (w_out_hbm, w_out))
    ):
        load = pltpu.make_async_copy(source, target, load_sem.at[k])
        load.start()
        loads.append(load)

    def partner(i):
        k = lax.rem(i, NZ)
        q = 7 - i // NZ
        dz = 4 + ((k + 1) // 2) * (1 - 2 * lax.rem(k, 2))
        return (
            lax.rem(sec + lax.rem(q, 2), SEC),
            lax.rem(z + dz, NZ),
            lax.rem(y + q // 2, NY),
        )

    line = [(sec, wrap(z + d, NZ), y, dp) for d in (4, 3, 5, 2, 6, 1, 7)]
    cross = [
        (sec, z, wrap(y + j, NY), wrap(dp + i, NX))
        for j in (2, 1, 3, 0)
        for i in (2, 1, 3, 0)
        if (i, j) != (0, 0)
    ]
    mate = [(1 - sec, z, y, dp)]
    plane = [
        (wrap(sec + s, SEC), z, wrap(y + j, NY), dp)
        for j in (2, 1, 3, 0)
        for s in (1, 0)
        if (s, j) != (0, 0)
    ]

    barrier = pltpu.get_barrier_semaphore()
    x_line = [(sec, z, y, wrap(dp + i, NX)) for i in (2, 1, 3)]
    greeted = line + plane + x_line
    for p in greeted:
        pl.semaphore_signal(barrier, inc=1, device_id=place(*p), device_id_type=MESH)

    slot_row = slot_ref[...]
    lane = lax.broadcasted_iota(I32, (64, LANES), 1)
    sub = lax.broadcasted_iota(I32, (64, LANES), 0)
    lane64 = lax.broadcasted_iota(I32, (64, 64), 1)
    sub64 = lax.broadcasted_iota(I32, (64, 64), 0)
    slot_col = jnp.sum(
        jnp.where(lane64 == sub64, jnp.broadcast_to(slot_row, (64, 64)), 0), axis=1, keepdims=True
    )
    hit = (slot_col >= lane * NBE) & (slot_col < lane * NBE + NBE)
    row_buf[0:1, :] = jnp.sum(jnp.where(hit, sub, 0), axis=0, keepdims=True)
    ids_row = jnp.sum(jnp.where(hit, slot_col + 1, 0), axis=0, keepdims=True) - 1
    tbl = pltpu.make_async_copy(row_buf.at[pl.ds(0, 1)], slot_tbl, tbl_sem.at[0])
    tbl.start()
    ids_line[z] = ids_row
    loads[0].wait()
    tbl.wait()

    def pack(d, carry):
        send[d] = llm[jnp.clip(slot_tbl[0, d], 0, 63)]
        return carry

    lax.fori_loop(0, SHARDS, pack, 0)
    recv[me] = send[me]

    pl.semaphore_wait(barrier, len(greeted))
    for p in plane:
        pl.semaphore_signal(lines_in, inc=1, device_id=place(*p), device_id_type=MESH)
    pl.semaphore_wait(lines_in, len(plane))

    def spread(partners, source, target_of, s_sem, r_sem):
        for i, p in enumerate(partners):
            pltpu.make_async_remote_copy(
                source, target_of(i), s_sem, r_sem, device_id=place(*p), device_id_type=MESH
            ).start()

    def wait_bytes(ref, sem):
        pltpu.make_async_copy(ref, ref, sem).wait()

    spread(line, ids_line.at[z], lambda i: ids_line.at[z], ids_send.at[0], ids_recv.at[0])

    def block_copy(i):
        s_at, z_at, y_at = partner(i)
        to = s_at * (NZ * NY) + z_at * NY + y_at
        return pltpu.make_async_remote_copy(
            send.at[to],
            recv.at[me],
            a2a_send.at[lax.rem(i, WIN)],
            a2a_recv,
            device_id=place(s_at, z_at, y_at, dp),
            device_id_type=MESH,
        )

    started = [0]
    ended = [0]

    def begin(count):
        low, high = started[0], min(SENDS, started[0] + count)
        started[0] = high
        assert high - ended[0] <= WIN

        def step(i, carry):
            block_copy(i).start()
            return carry

        if high > low:
            lax.fori_loop(low, high, step, 0)

    def settle(left):
        low, high = ended[0], max(ended[0], started[0] - left)
        ended[0] = high

        def step(i, carry):
            block_copy(i).wait_send()
            return carry

        if high > low:
            lax.fori_loop(low, high, step, 0)

    def reserve(count):
        first = (ended[0], started[0])
        ended[0] += count
        started[0] += count
        assert started[0] <= SENDS
        return first

    def pump(first, i):
        block_copy(first[0] + i).wait_send()
        block_copy(first[1] + i).start()

    begin(8)

    loads[1].wait()
    gain = ln_gain_ref[...]
    bias = ln_bias_ref[...]

    def norm(r, carry):
        rows = pl.ds(pl.multiple_of(r * 64, 64), 64)
        values = enc[rows, :].astype(F32)
        mean = jnp.mean(values, axis=1, keepdims=True)
        centred = values - mean
        scale = lax.rsqrt(jnp.mean(centred * centred, axis=1, keepdims=True) + EPS)
        hat = centred * scale
        rstd[rows, :] = jnp.broadcast_to(scale, (64, LANES))
        x_hat[rows, :] = hat
        normed[rows, :] = (hat * gain + bias).astype(BF16)
        return carry

    lax.fori_loop(0, 8, norm, 0)
    begin(2)

    loads[2].wait()
    moved = reserve(4)

    def project(n, carry):
        at = pl.ds(pl.multiple_of(n * 256, 256), 256)
        gate_at = pl.ds(pl.multiple_of(C + n * 256, 256), 256)
        lin = jnp.dot(normed[...], w_in[:, at], preferred_element_type=F32)
        gate = jnp.dot(normed[...], w_in[:, gate_at], preferred_element_type=F32)
        pump(moved, n)
        s = jax.nn.sigmoid(gate)
        mixed = lin * s
        sig[:, at] = s
        dsig[:, at] = mixed * (1.0 - s)
        gated[pl.ds(PAD, FRAMES), at] = mixed.astype(BF16).astype(F32)
        return carry

    lax.fori_loop(0, 4, project, 0)

    before = wrap(me + SHARDS - 1, SHARDS)
    after = wrap(me + 1, SHARDS)

    def edges(buf, k):
        for j, (to, start, end) in enumerate(
            ((after, FRAMES, 0), (before, PAD, PAD + FRAMES))
        ):
            pltpu.make_async_remote_copy(
                buf.at[pl.ds(start, PAD)],
                buf.at[pl.ds(end, PAD)],
                halo_send.at[k, j],
                halo_recv.at[k, j],
                device_id={"sec": to // (NZ * NY), "tm": lax.rem(to, NZ * NY), "dp": dp},
                device_id_type=MESH,
            ).start()

    def edges_in(buf, k):
        wait_bytes(buf.at[pl.ds(0, PAD)], halo_recv.at[k, 0])
        wait_bytes(buf.at[pl.ds(PAD + FRAMES, PAD)], halo_recv.at[k, 1])

    def edges_out(buf, k):
        wait_bytes(buf.at[pl.ds(0, PAD)], halo_send.at[k, 0])
        wait_bytes(buf.at[pl.ds(0, PAD)], halo_send.at[k, 1])

    settle(6)
    edges(gated, 0)
    begin(6)

    wait_bytes(ids_line.at[pl.ds(0, NZ - 1)], ids_recv.at[0])
    for j in range(NZ):
        ids_tile[j : j + 1, :] = ids_line[j]
    here = sec * NY + y
    ids_all[here] = ids_tile[...]
    spread(plane, ids_tile, lambda i: ids_all.at[here], ids_send.at[1], ids_recv.at[1])

    utt_pad[...] = jnp.zeros((8, UTT_PAD), I32)
    utt_pad[0:1, 0:UTT] = utt_ref[...]
    lengths = utt_pad[...].astype(F32).astype(BF16)
    upper = (
        lax.broadcasted_iota(I32, (UTT_PAD, UTT_PAD), 0)
        <= lax.broadcasted_iota(I32, (UTT_PAD, UTT_PAD), 1)
    ).astype(F32).astype(BF16)
    ends = jnp.dot(lengths, upper, preferred_element_type=F32)[0:1, :]

    def number(r, carry):
        rows = pl.ds(pl.multiple_of(r * 48, 8), 48)
        position = lax.broadcasted_iota(I32, (48, 1), 0) + (r * 48 + me * FRAMES - PAD)
        position_f = position.astype(F32)
        count = jnp.sum((position_f >= ends).astype(F32), axis=1, keepdims=True)
        inside = (position >= 0) & (position < SHARDS * FRAMES)
        seg[rows, :] = jnp.broadcast_to(jnp.where(inside, count, -1.0), (48, LANES))
        return carry

    lax.fori_loop(0, EXT // 48, number, 0)

    def mark(r, carry):
        window = seg[pl.ds(pl.multiple_of(r * ROWS, ROWS), ROWS + 2 * PAD), :]
        own = window[PAD : PAD + ROWS]
        rows = pl.ds(pl.multiple_of(r * ROWS, ROWS), ROWS)
        for j in range(TAPS):
            masks[j, rows, :] = (window[HALF + j : HALF + j + ROWS] == own).astype(F32)
        return carry

    lax.fori_loop(0, FRAMES // ROWS, mark, 0)
    edges_in(gated, 0)

    moved_conv = reserve(8)

    def convolve(c, carry):
        cols = pl.ds(pl.multiple_of(c * LANES, LANES), LANES)
        taps = dw_ref[:, cols]
        first_sum = jnp.zeros((1, LANES), F32)
        second_sum = jnp.zeros((1, LANES), F32)
        for r in range(FRAMES // ROWS):
            window = gated[r * ROWS : r * ROWS + ROWS + 2 * PAD, cols]
            total = jnp.zeros((ROWS, LANES), F32)
            for k in range(TAPS):
                part = window[HALF + k : HALF + k + ROWS]
                if k != HALF:
                    part = part * masks[k, r * ROWS : r * ROWS + ROWS, :]
                total = total + taps[k : k + 1, :] * part
            conv[PAD + r * ROWS : PAD + r * ROWS + ROWS, cols] = total
            first_sum = first_sum + jnp.sum(total, axis=0, keepdims=True)
            second_sum = second_sum + jnp.sum(total * total, axis=0, keepdims=True)
        ar_src[0, 0, 0, pl.ds(c, 1), :] = first_sum
        ar_src[0, 0, 1, pl.ds(c, 1), :] = second_sum
        pump(moved_conv, c)
        return carry

    lax.fori_loop(0, COLS, convolve, 0)
    groups = ((mate, ar_s), (cross, ar_xy), (line, ar_z))

    def sum_send(k, step):
        partners, target = groups[step]
        spread(
            partners,
            ar_src.at[k, step],
            lambda i: target.at[k, i],
            ar_send.at[k, step],
            ar_recv.at[k, step],
        )

    def sum_recv(k, step):
        partners, target = groups[step]
        count = len(partners)
        wait_bytes(target.at[k, pl.ds(0, count)], ar_recv.at[k, step])
        total = ar_src[k, step]
        for i in range(count):
            total = total + target[k, i]
        ar_src[k, step + 1] = total

    def sum_done(k):
        for step, (partners, target) in enumerate(groups):
            wait_bytes(target.at[k, pl.ds(0, len(partners))], ar_send.at[k, step])

    settle(4)
    sum_send(0, 0)
    edges(conv, 1)
    begin(7)
    sum_recv(0, 0)
    for step in (1, 2):
        settle(4)
        sum_send(0, step)
        begin(8)
        sum_recv(0, step)

    wait_bytes(ids_all.at[pl.ds(0, 7)], ids_recv.at[1])
    ids = ids_all[...].reshape(64, LANES)
    mine = jnp.sum(jnp.where(lane == me, ids, 0), axis=1, keepdims=True) - me * NBE
    quarter = sub // NZ
    source = (quarter // NY) * (NZ * NY) + lax.rem(sub, NZ) * NY + lax.rem(quarter, NY)
    row_buf[1:2, :] = jnp.sum(jnp.where(mine == lane, source, 0), axis=0, keepdims=True)
    src_copy = pltpu.make_async_copy(row_buf.at[pl.ds(1, 1)], src_tbl, tbl_sem.at[1])
    src_copy.start()

    edges_in(conv, 1)
    edges_out(conv, 1)

    moved_bn = reserve(8)

    def bn_scales(c):
        bn_mean = ar_src[0, 3, 0, pl.ds(c, 1), :] / ALL_FRAMES
        bn_var = ar_src[0, 3, 1, pl.ds(c, 1), :] / ALL_FRAMES - bn_mean * bn_mean
        return bn_mean, lax.rsqrt(bn_var + EPS)

    def normalise(c, carry):
        cols = pl.ds(pl.multiple_of(c * LANES, LANES), LANES)
        bn_mean, bn_rstd = bn_scales(c)
        bn_gain = bn_gain_ref[pl.ds(c, 1), :]
        bn_bias = bn_bias_ref[pl.ds(c, 1), :]
        taps = dw_ref[:, cols]
        factor = bn_gain * bn_rstd
        for r in range(EXT // 48):
            rows = slice(r * 48, r * 48 + 48)
            conv[rows, cols] = (conv[rows, cols] - bn_mean) * bn_rstd
        for r in range(FRAMES // ROWS):
            rows = slice(r * ROWS, r * ROWS + ROWS)
            window = conv[r * ROWS : r * ROWS + ROWS + 2 * PAD, cols]
            pre = window[PAD : PAD + ROWS] * bn_gain + bn_bias
            s = jax.nn.sigmoid(pre)
            swish[rows, cols] = s * (1.0 + pre * (1.0 - s))
            ones_total = jnp.zeros((ROWS, LANES), F32)
            z_total = jnp.zeros((ROWS, LANES), F32)
            for j in range(TAPS):
                weight = (taps[TAPS - 1 - j : TAPS - j, :] * factor) * masks[j, rows, :]
                ones_total = ones_total + weight
                z_total = z_total + weight * window[HALF + j : HALF + j + ROWS]
            ones_t[rows, cols] = ones_total
            z_t[rows, cols] = z_total
        pump(moved_bn, c)
        return carry

    lax.fori_loop(0, COLS, normalise, 0)
    src_copy.wait()
    loads[3].wait()
    settle(WIN - (SENDS - started[0]))
    begin(SENDS)
    assert started[0] == SENDS

    wait_bytes(recv.at[pl.ds(0, SENDS)], a2a_recv)

    def gather(b, carry):
        inc[pl.ds(pl.multiple_of(b * BLK, BLK), BLK), :] = recv[jnp.clip(src_tbl[0, b], 0, 63)]
        return carry

    lax.fori_loop(0, NBE, gather, 0)

    for n in range(4):
        at = slice(n * 256, n * 256 + 256)
        grad = lax.dot_general(inc[...], w_out[at, :], NT, preferred_element_type=F32)
        grad = grad * swish[:, at]
        d_pre[PAD : PAD + FRAMES, at] = grad
        first_sum = jnp.sum(grad, axis=0, keepdims=True)
        cross_sum = jnp.sum(grad * conv[PAD : PAD + FRAMES, at], axis=0, keepdims=True)
        for j in range(2):
            c = 2 * n + j
            ar_src[1, 0, 0, c : c + 1, :] = first_sum[:, j * LANES : (j + 1) * LANES]
            ar_src[1, 0, 1, c : c + 1, :] = cross_sum[:, j * LANES : (j + 1) * LANES]

    def conv_back(c, carry):
        cols = pl.ds(pl.multiple_of(c * LANES, LANES), LANES)
        bn_mean, bn_rstd = bn_scales(c)
        factor = bn_gain_ref[pl.ds(c, 1), :] * bn_rstd
        taps = dw_ref[:, cols] * factor
        for r in range(FRAMES // ROWS):
            rows = slice(r * ROWS, r * ROWS + ROWS)
            window = d_pre[r * ROWS : r * ROWS + ROWS + 2 * PAD, cols]
            total = jnp.zeros((ROWS, LANES), F32)
            for j in range(TAPS):
                part = window[HALF + j : HALF + j + ROWS]
                if j != HALF:
                    part = part * masks[j, rows, :]
                total = total + taps[TAPS - 1 - j : TAPS - j, :] * part
            d_t[rows, cols] = total
        return carry

    sum_send(1, 0)
    edges(d_pre, 2)
    sum_recv(1, 0)
    sum_send(1, 1)
    edges_in(d_pre, 2)
    lax.fori_loop(0, COLS // 2, conv_back, 0)
    sum_recv(1, 1)
    sum_send(1, 2)
    lax.fori_loop(COLS // 2, COLS, conv_back, 0)
    sum_recv(1, 2)

    def assemble(c, carry):
        cols = pl.ds(pl.multiple_of(c * LANES, LANES), LANES)
        gate_cols = pl.ds(pl.multiple_of(C + c * LANES, LANES), LANES)
        grad_mean = ar_src[1, 3, 0, pl.ds(c, 1), :] / ALL_FRAMES
        cross_mean = ar_src[1, 3, 1, pl.ds(c, 1), :] / ALL_FRAMES
        for r in range(FRAMES // ROWS):
            rows = slice(r * ROWS, r * ROWS + ROWS)
            grad = d_t[rows, cols] - grad_mean * ones_t[rows, cols] - cross_mean * z_t[rows, cols]
            d_mixed[rows, cols] = (grad * sig[rows, cols]).astype(BF16)
            d_mixed[rows, gate_cols] = (grad * dsig[rows, cols]).astype(BF16)
        return carry

    lax.fori_loop(0, COLS, assemble, 0)

    for n in range(4):
        at = slice(n * 256, n * 256 + 256)
        grad = lax.dot_general(d_mixed[...], w_in[at, :], NT, preferred_element_type=F32)
        h_buf[:, at] = grad * ln_gain_ref[:, at]

    def finish(k, carry):
        part = pl.ds(pl.multiple_of(k * 32, 32), 32)
        h = h_buf[part, :]
        hat = x_hat[part, :]
        mean = jnp.mean(h, axis=1, keepdims=True)
        along = jnp.mean(h * hat, axis=1, keepdims=True)
        scale = rstd[part, 0:1]
        out_ref[part, :] = (inc[part, :].astype(F32) + scale * (h - mean - hat * along)).astype(BF16)
        return carry

    lax.fori_loop(0, FRAMES // 32, finish, 0)

    settle(0)
    wait_bytes(ids_line.at[pl.ds(0, NZ - 1)], ids_send.at[0])
    wait_bytes(ids_all.at[pl.ds(0, 7)], ids_send.at[1])
    edges_out(gated, 0)
    edges_out(d_pre, 2)
    sum_done(0)
    sum_done(1)


def local(
    enc_input,
    llm_grads,
    slot_block,
    utt_lengths,
    ln_gain,
    ln_bias,
    w_in,
    dw_kernel,
    bn_gain,
    bn_bias,
    w_out,
):
    vmem = pl.BlockSpec(memory_space=pltpu.VMEM)
    hbm = pl.BlockSpec(memory_space=pl.ANY)
    dma = pltpu.SemaphoreType.DMA
    full = pltpu.VMEM((FRAMES, C), F32)
    wide = pltpu.VMEM((EXT, C), F32)
    blocks = pltpu.VMEM((SHARDS, BLK, C), BF16)
    out = pl.pallas_call(
        kernel,
        out_shape=jax.ShapeDtypeStruct((FRAMES, C), BF16),
        in_specs=[hbm] * 4 + [vmem] * 7,
        out_specs=vmem,
        scratch_shapes=[
            pltpu.VMEM((FRAMES, C), BF16),
            blocks,
            pltpu.VMEM((C, 2 * C), BF16),
            pltpu.VMEM((C, C), BF16),
            blocks,
            blocks,
            pltpu.VMEM((8, LANES), I32),
            pltpu.SMEM((1, LANES), I32),
            pltpu.SMEM((1, LANES), I32),
            pltpu.VMEM((NZ, 1, LANES), I32),
            pltpu.VMEM((NZ, LANES), I32),
            pltpu.VMEM((8, NZ, LANES), I32),
            pltpu.VMEM((8, UTT_PAD), I32),
            pltpu.VMEM((EXT, LANES), F32),
            pltpu.VMEM((TAPS, FRAMES, LANES), F32),
            full,
            pltpu.VMEM((FRAMES, LANES), F32),
            pltpu.VMEM((FRAMES, C), BF16),
            full,
            full,
            wide,
            wide,
            full,
            full,
            full,
            full,
            wide,
            pltpu.VMEM((FRAMES, C), BF16),
            pltpu.VMEM((FRAMES, 2 * C), BF16),
            full,
            pltpu.VMEM((2, 4, 2, COLS, LANES), F32),
            pltpu.VMEM((2, 1, 2, COLS, LANES), F32),
            pltpu.VMEM((2, 15, 2, COLS, LANES), F32),
            pltpu.VMEM((2, 7, 2, COLS, LANES), F32),
            dma((4,)),
            dma((2,)),
            dma((WIN,)),
            dma,
            dma((2,)),
            dma((2,)),
            dma((3, 2)),
            dma((3, 2)),
            dma((2, 3)),
            dma((2, 3)),
            pltpu.SemaphoreType.REGULAR,
        ],
        compiler_params=pltpu.CompilerParams(
            collective_id=1, has_side_effects=True, vmem_limit_bytes=56 << 20
        ),
        name="conv_module_back",
    )(
        enc_input[0],
        llm_grads[0].reshape(SHARDS, BLK, C),
        w_in,
        w_out,
        slot_block,
        utt_lengths,
        ln_gain.reshape(1, C),
        ln_bias.reshape(1, C),
        dw_kernel,
        bn_gain.reshape(COLS, LANES),
        bn_bias.reshape(COLS, LANES),
    )
    return out[None]


def solution(mesh):
    in_specs = (
        P("dp", ("sec", "tm"), None),
        P("dp", ("sec", "tm"), None),
        P("dp", ("sec", "tm")),
        P("dp", None),
        P(),
        P(),
        P(),
        P(),
        P(),
        P(),
        P(),
    )
    out_specs = P("dp", ("sec", "tm"), None)
    return jax.shard_map(local, mesh=mesh, in_specs=in_specs, out_specs=out_specs, check_vma=False)
```

```python
import functools

import jax
import jax.numpy as jnp
from jax import lax
from jax.experimental import pallas as pl
from jax.experimental.pallas import tpu as pltpu
from jax.sharding import PartitionSpec as P

MESH = pl.DeviceIdType.MESH
F32 = jnp.float32
BF16 = jnp.bfloat16
I32 = jnp.int32

EPS = 1e-05
SEC, NZ, NY, NX = 2, 8, 4, 4
SHARDS = SEC * NZ * NY
FRAMES = 512
C = 1024
TAPS = 9
HALF = 4
PAD = 8
EXT = FRAMES + 2 * PAD
EDGE = 16
THIRD = EXT // 3
WIDE = FRAMES + 2 * EDGE
BLK = 16
NBE = 32
UTT = 262
UTT_PAD = 384
LANES = 128
COLS = C // LANES
ROWS = 128
WIN = 20
SENDS = SHARDS - 1
ALL_FRAMES = float(FRAMES * SHARDS * NX)
NT = (((1,), (1,)), ((), ()))


def wrap(value, count):
    return lax.rem(value + count, count)


def kernel(
    enc_hbm,
    llm_hbm,
    w_in_hbm,
    w_out_hbm,
    slot_ref,
    utt_ref,
    ln_gain_ref,
    ln_bias_ref,
    dw_ref,
    bn_gain_ref,
    bn_bias_ref,
    out_hbm,
    enc,
    llm,
    w_in,
    w_out,
    send,
    recv,
    row_buf,
    slot_tbl,
    src_tbl,
    ids_line,
    ids_tile,
    ids_all,
    utt_pad,
    seg,
    masks,
    x_hat,
    rstd,
    normed,
    sig,
    dsig,
    gated,
    conv,
    swish,
    ones_t,
    z_t,
    d_t,
    d_pre,
    inc,
    d_mixed,
    out_buf,
    ar_src,
    ar_s,
    ar_xy,
    ar_z,
    load_sem,
    tbl_sem,
    a2a_send,
    a2a_recv,
    ids_send,
    ids_recv,
    halo_send,
    halo_recv,
    ar_send,
    ar_recv,
    out_sem,
    lines_in,
):
    sec = lax.axis_index("sec")
    tm = lax.axis_index("tm")
    dp = lax.axis_index("dp")
    z = tm // NY
    y = lax.rem(tm, NY)
    me = sec * (NZ * NY) + tm

    def place(s_at, z_at, y_at, x_at):
        return {"sec": s_at, "tm": z_at * NY + y_at, "dp": x_at}

    loads = []
    for k, (source, target) in enumerate(
        ((llm_hbm, llm), (enc_hbm, enc.at[pl.ds(EDGE, FRAMES)]), (w_in_hbm, w_in), (w_out_hbm, w_out))
    ):
        load = pltpu.make_async_copy(source, target, load_sem.at[k])
        load.start()
        loads.append(load)

    def partner(i):
        k = lax.rem(i, NZ)
        q = 7 - i // NZ
        dz = 4 + ((k + 1) // 2) * (1 - 2 * lax.rem(k, 2))
        return (
            lax.rem(sec + lax.rem(q, 2), SEC),
            lax.rem(z + dz, NZ),
            lax.rem(y + q // 2, NY),
        )

    line = [(sec, wrap(z + d, NZ), y, dp) for d in (4, 3, 5, 2, 6, 1, 7)]
    cross = [
        (sec, z, wrap(y + j, NY), wrap(dp + i, NX))
        for j in (2, 1, 3, 0)
        for i in (2, 1, 3, 0)
        if (i, j) != (0, 0)
    ]
    mate = [(1 - sec, z, y, dp)]
    plane = [
        (wrap(sec + s, SEC), z, wrap(y + j, NY), dp)
        for j in (2, 1, 3, 0)
        for s in (1, 0)
        if (s, j) != (0, 0)
    ]

    barrier = pltpu.get_barrier_semaphore()
    x_line = [(sec, z, y, wrap(dp + i, NX)) for i in (2, 1, 3)]
    greeted = line + plane + x_line
    for p in greeted:
        pl.semaphore_signal(barrier, inc=1, device_id=place(*p), device_id_type=MESH)

    slot_row = slot_ref[...]
    lane = lax.broadcasted_iota(I32, (64, LANES), 1)
    sub = lax.broadcasted_iota(I32, (64, LANES), 0)
    lane64 = lax.broadcasted_iota(I32, (64, 64), 1)
    sub64 = lax.broadcasted_iota(I32, (64, 64), 0)
    slot_col = jnp.sum(
        jnp.where(lane64 == sub64, jnp.broadcast_to(slot_row, (64, 64)), 0), axis=1, keepdims=True
    )
    hit = (slot_col >= lane * NBE) & (slot_col < lane * NBE + NBE)
    row_buf[0:1, :] = jnp.sum(jnp.where(hit, sub, 0), axis=0, keepdims=True)
    ids_row = jnp.sum(jnp.where(hit, slot_col + 1, 0), axis=0, keepdims=True) - 1
    tbl = pltpu.make_async_copy(row_buf.at[pl.ds(0, 1)], slot_tbl, tbl_sem.at[0])
    tbl.start()
    ids_line[z] = ids_row
    loads[0].wait()
    tbl.wait()

    def pack(d, carry):
        send[d] = llm[jnp.clip(slot_tbl[0, d], 0, 63)]
        return carry

    lax.fori_loop(0, SHARDS, pack, 0)
    recv[me] = send[me]

    pl.semaphore_wait(barrier, len(greeted))
    for p in plane:
        pl.semaphore_signal(lines_in, inc=1, device_id=place(*p), device_id_type=MESH)
    pl.semaphore_wait(lines_in, len(plane))

    def spread(partners, source, target_of, s_sem, r_sem):
        for i, p in enumerate(partners):
            pltpu.make_async_remote_copy(
                source, target_of(i), s_sem, r_sem, device_id=place(*p), device_id_type=MESH
            ).start()

    def wait_bytes(ref, sem):
        pltpu.make_async_copy(ref, ref, sem).wait()

    before = wrap(me + SHARDS - 1, SHARDS)
    after = wrap(me + 1, SHARDS)

    def edges(buf, rows, k):
        for j, (to, start, end) in enumerate(
            ((after, FRAMES, 0), (before, rows, rows + FRAMES))
        ):
            pltpu.make_async_remote_copy(
                buf.at[pl.ds(start, rows)],
                buf.at[pl.ds(end, rows)],
                halo_send.at[k, j],
                halo_recv.at[k, j],
                device_id={"sec": to // (NZ * NY), "tm": lax.rem(to, NZ * NY), "dp": dp},
                device_id_type=MESH,
            ).start()

    def edges_in(buf, rows, k):
        wait_bytes(buf.at[pl.ds(0, rows)], halo_recv.at[k, 0])
        wait_bytes(buf.at[pl.ds(0, rows)], halo_recv.at[k, 1])

    def edges_out(buf, rows, k):
        wait_bytes(buf.at[pl.ds(0, rows)], halo_send.at[k, 0])
        wait_bytes(buf.at[pl.ds(0, rows)], halo_send.at[k, 1])

    loads[1].wait()
    edges(enc, EDGE, 0)
    spread(line, ids_line.at[z], lambda i: ids_line.at[z], ids_send.at[0], ids_recv.at[0])

    def block_copy(i):
        s_at, z_at, y_at = partner(i)
        to = s_at * (NZ * NY) + z_at * NY + y_at
        return pltpu.make_async_remote_copy(
            send.at[to],
            recv.at[me],
            a2a_send.at[lax.rem(i, WIN)],
            a2a_recv,
            device_id=place(s_at, z_at, y_at, dp),
            device_id_type=MESH,
        )

    started = [0]
    ended = [0]

    def begin(count):
        low, high = started[0], min(SENDS, started[0] + count)
        started[0] = high
        assert high - ended[0] <= WIN

        def step(i, carry):
            block_copy(i).start()
            return carry

        if high > low:
            lax.fori_loop(low, high, step, 0)

    def settle(left):
        low, high = ended[0], max(ended[0], started[0] - left)
        ended[0] = high

        def step(i, carry):
            block_copy(i).wait_send()
            return carry

        if high > low:
            lax.fori_loop(low, high, step, 0)

    def reserve(count):
        first = (ended[0], started[0])
        ended[0] += count
        started[0] += count
        assert started[0] <= SENDS
        return first

    def pump(first, i):
        block_copy(first[0] + i).wait_send()
        block_copy(first[1] + i).start()

    begin(10)

    gain = ln_gain_ref[...]
    bias = ln_bias_ref[...]

    def norm_rows(values):
        values = values.astype(F32)
        mean = jnp.mean(values, axis=1, keepdims=True)
        centred = values - mean
        scale = lax.rsqrt(jnp.mean(centred * centred, axis=1, keepdims=True) + EPS)
        hat = centred * scale
        return hat, scale, (hat * gain + bias).astype(BF16)

    def norm(r, carry):
        rows = pl.ds(pl.multiple_of(r * 64, 64), 64)
        wide_rows = pl.ds(pl.multiple_of(r * 64 + EDGE, EDGE), 64)
        hat, scale, out = norm_rows(enc[wide_rows, :])
        rstd[rows, :] = jnp.broadcast_to(scale, (64, LANES))
        x_hat[rows, :] = hat
        normed[wide_rows, :] = out
        return carry

    lax.fori_loop(0, 8, norm, 0)

    utt_pad[...] = jnp.zeros((8, UTT_PAD), I32)
    utt_pad[0:1, 0:UTT] = utt_ref[...]
    lengths = utt_pad[...].astype(F32).astype(BF16)
    upper = (
        lax.broadcasted_iota(I32, (UTT_PAD, UTT_PAD), 0)
        <= lax.broadcasted_iota(I32, (UTT_PAD, UTT_PAD), 1)
    ).astype(F32).astype(BF16)
    ends = jnp.dot(lengths, upper, preferred_element_type=F32)[0:1, :]

    def number(r, carry):
        rows = pl.ds(pl.multiple_of(r * 136, 8), 136)
        position = lax.broadcasted_iota(I32, (136, 1), 0) + (r * 136 + me * FRAMES - EDGE)
        position_f = position.astype(F32)
        count = jnp.sum((position_f >= ends).astype(F32), axis=1, keepdims=True)
        inside = (position >= 0) & (position < SHARDS * FRAMES)
        seg[rows, :] = jnp.broadcast_to(jnp.where(inside, count, -1.0), (136, LANES))
        return carry

    lax.fori_loop(0, WIDE // 136, number, 0)

    def mark(r, carry):
        window = seg[pl.ds(pl.multiple_of(r * THIRD, 16), THIRD + 2 * PAD), :]
        own = window[PAD : PAD + THIRD]
        rows = pl.ds(pl.multiple_of(r * THIRD, 16), THIRD)
        for j in range(TAPS):
            masks[j, rows, :] = (window[HALF + j : HALF + j + THIRD] == own).astype(F32)
        return carry

    lax.fori_loop(0, EXT // THIRD, mark, 0)

    edges_in(enc, EDGE, 0)
    for start in (0, EDGE + FRAMES):
        normed[start : start + EDGE, :] = norm_rows(enc[start : start + EDGE, :])[2]

    loads[2].wait()
    moved = reserve(4)

    def project(n, carry):
        at = pl.ds(pl.multiple_of(n * 256, 256), 256)
        gate_at = pl.ds(pl.multiple_of(C + n * 256, 256), 256)
        lin = jnp.dot(normed[...], w_in[:, at], preferred_element_type=F32)
        gate = jnp.dot(normed[...], w_in[:, gate_at], preferred_element_type=F32)
        pump(moved, n)
        s = jax.nn.sigmoid(gate)
        mixed = lin * s
        sig[:, at] = s[EDGE : EDGE + FRAMES]
        dsig[:, at] = (mixed * (1.0 - s))[EDGE : EDGE + FRAMES]
        gated[:, at] = mixed.astype(BF16).astype(F32)
        return carry

    lax.fori_loop(0, 4, project, 0)

    moved_conv = reserve(8)

    def convolve(c, carry):
        cols = pl.ds(pl.multiple_of(c * LANES, LANES), LANES)
        taps = dw_ref[:, cols]
        first_sum = jnp.zeros((1, LANES), F32)
        second_sum = jnp.zeros((1, LANES), F32)
        for r in range(EXT // THIRD):
            window = gated[r * THIRD : r * THIRD + THIRD + 2 * PAD, cols]
            total = jnp.zeros((THIRD, LANES), F32)
            for k in range(TAPS):
                part = window[HALF + k : HALF + k + THIRD]
                if k != HALF:
                    part = part * masks[k, r * THIRD : r * THIRD + THIRD, :]
                total = total + taps[k : k + 1, :] * part
            conv[r * THIRD : r * THIRD + THIRD, cols] = total
            own = total[(PAD if r == 0 else 0) : (THIRD - PAD if r == EXT // THIRD - 1 else THIRD)]
            first_sum = first_sum + jnp.sum(own, axis=0, keepdims=True)
            second_sum = second_sum + jnp.sum(own * own, axis=0, keepdims=True)
        ar_src[0, 0, 0, pl.ds(c, 1), :] = first_sum
        ar_src[0, 0, 1, pl.ds(c, 1), :] = second_sum
        pump(moved_conv, c)
        return carry

    lax.fori_loop(0, COLS, convolve, 0)

    groups = ((mate, ar_s), (cross, ar_xy), (line, ar_z))

    def sum_send(k, step):
        partners, target = groups[step]
        spread(
            partners,
            ar_src.at[k, step],
            lambda i: target.at[k, i],
            ar_send.at[k, step],
            ar_recv.at[k, step],
        )

    def sum_recv(k, step):
        partners, target = groups[step]
        count = len(partners)
        wait_bytes(target.at[k, pl.ds(0, count)], ar_recv.at[k, step])
        total = ar_src[k, step]
        for i in range(count):
            total = total + target[k, i]
        ar_src[k, step + 1] = total

    def sum_done(k):
        for step, (partners, target) in enumerate(groups):
            wait_bytes(target.at[k, pl.ds(0, len(partners))], ar_send.at[k, step])

    settle(8)
    sum_send(0, 0)
    begin(8)

    wait_bytes(ids_line.at[pl.ds(0, NZ - 1)], ids_recv.at[0])
    for j in range(NZ):
        ids_tile[j : j + 1, :] = ids_line[j]
    here = sec * NY + y
    ids_all[here] = ids_tile[...]
    spread(plane, ids_tile, lambda i: ids_all.at[here], ids_send.at[1], ids_recv.at[1])

    sum_recv(0, 0)
    settle(6)
    sum_send(0, 1)
    begin(12)
    sum_recv(0, 1)
    settle(6)
    sum_send(0, 2)
    begin(12)
    sum_recv(0, 2)

    wait_bytes(ids_all.at[pl.ds(0, 7)], ids_recv.at[1])
    ids = ids_all[...].reshape(64, LANES)
    mine = jnp.sum(jnp.where(lane == me, ids, 0), axis=1, keepdims=True) - me * NBE
    quarter = sub // NZ
    source = (quarter // NY) * (NZ * NY) + lax.rem(sub, NZ) * NY + lax.rem(quarter, NY)
    row_buf[1:2, :] = jnp.sum(jnp.where(mine == lane, source, 0), axis=0, keepdims=True)
    src_copy = pltpu.make_async_copy(row_buf.at[pl.ds(1, 1)], src_tbl, tbl_sem.at[1])
    src_copy.start()

    moved_bn = reserve(8)

    def bn_scales(c):
        bn_mean = ar_src[0, 3, 0, pl.ds(c, 1), :] / ALL_FRAMES
        bn_var = ar_src[0, 3, 1, pl.ds(c, 1), :] / ALL_FRAMES - bn_mean * bn_mean
        return bn_mean, lax.rsqrt(bn_var + EPS)

    def normalise(c, carry):
        cols = pl.ds(pl.multiple_of(c * LANES, LANES), LANES)
        bn_mean, bn_rstd = bn_scales(c)
        bn_gain = bn_gain_ref[pl.ds(c, 1), :]
        bn_bias = bn_bias_ref[pl.ds(c, 1), :]
        taps = dw_ref[:, cols]
        factor = bn_gain * bn_rstd
        for r in range(EXT // 48):
            rows = slice(r * 48, r * 48 + 48)
            conv[rows, cols] = (conv[rows, cols] - bn_mean) * bn_rstd
        for r in range(FRAMES // ROWS):
            rows = slice(r * ROWS, r * ROWS + ROWS)
            window = conv[r * ROWS : r * ROWS + ROWS + 2 * PAD, cols]
            pre = window[PAD : PAD + ROWS] * bn_gain + bn_bias
            s = jax.nn.sigmoid(pre)
            swish[rows, cols] = s * (1.0 + pre * (1.0 - s))
            ones_total = jnp.zeros((ROWS, LANES), F32)
            z_total = jnp.zeros((ROWS, LANES), F32)
            for j in range(TAPS):
                weight = (taps[TAPS - 1 - j : TAPS - j, :] * factor) * masks[j, PAD + r * ROWS : PAD + r * ROWS + ROWS, :]
                ones_total = ones_total + weight
                z_total = z_total + weight * window[HALF + j : HALF + j + ROWS]
            ones_t[rows, cols] = ones_total
            z_t[rows, cols] = z_total
        pump(moved_bn, c)
        return carry

    lax.fori_loop(0, COLS, normalise, 0)
    src_copy.wait()
    loads[3].wait()
    settle(WIN - (SENDS - started[0]))
    begin(SENDS)
    assert started[0] == SENDS

    wait_bytes(recv.at[pl.ds(0, SENDS)], a2a_recv)

    def gather(b, carry):
        inc[pl.ds(pl.multiple_of(b * BLK, BLK), BLK), :] = recv[jnp.clip(src_tbl[0, b], 0, 63)]
        return carry

    lax.fori_loop(0, NBE, gather, 0)

    for n in range(4):
        at = slice(n * 256, n * 256 + 256)
        grad = lax.dot_general(inc[...], w_out[at, :], NT, preferred_element_type=F32)
        grad = grad * swish[:, at]
        d_pre[PAD : PAD + FRAMES, at] = grad
        first_sum = jnp.sum(grad, axis=0, keepdims=True)
        cross_sum = jnp.sum(grad * conv[PAD : PAD + FRAMES, at], axis=0, keepdims=True)
        for j in range(2):
            c = 2 * n + j
            ar_src[1, 0, 0, c : c + 1, :] = first_sum[:, j * LANES : (j + 1) * LANES]
            ar_src[1, 0, 1, c : c + 1, :] = cross_sum[:, j * LANES : (j + 1) * LANES]

    def conv_back(c, carry):
        cols = pl.ds(pl.multiple_of(c * LANES, LANES), LANES)
        bn_mean, bn_rstd = bn_scales(c)
        factor = bn_gain_ref[pl.ds(c, 1), :] * bn_rstd
        taps = dw_ref[:, cols] * factor
        for r in range(FRAMES // ROWS):
            rows = slice(r * ROWS, r * ROWS + ROWS)
            window = d_pre[r * ROWS : r * ROWS + ROWS + 2 * PAD, cols]
            total = jnp.zeros((ROWS, LANES), F32)
            for j in range(TAPS):
                part = window[HALF + j : HALF + j + ROWS]
                if j != HALF:
                    part = part * masks[j, PAD + r * ROWS : PAD + r * ROWS + ROWS, :]
                total = total + taps[TAPS - 1 - j : TAPS - j, :] * part
            d_t[rows, cols] = total
        return carry

    sum_send(1, 0)
    edges(d_pre, PAD, 1)
    sum_recv(1, 0)
    sum_send(1, 1)
    edges_in(d_pre, PAD, 1)
    lax.fori_loop(0, COLS // 2, conv_back, 0)
    sum_recv(1, 1)
    sum_send(1, 2)
    lax.fori_loop(COLS // 2, COLS, conv_back, 0)
    sum_recv(1, 2)

    def assemble(c, carry):
        cols = pl.ds(pl.multiple_of(c * LANES, LANES), LANES)
        gate_cols = pl.ds(pl.multiple_of(C + c * LANES, LANES), LANES)
        grad_mean = ar_src[1, 3, 0, pl.ds(c, 1), :] / ALL_FRAMES
        cross_mean = ar_src[1, 3, 1, pl.ds(c, 1), :] / ALL_FRAMES
        for r in range(FRAMES // ROWS):
            rows = slice(r * ROWS, r * ROWS + ROWS)
            grad = d_t[rows, cols] - grad_mean * ones_t[rows, cols] - cross_mean * z_t[rows, cols]
            d_mixed[rows, cols] = (grad * sig[rows, cols]).astype(BF16)
            d_mixed[rows, gate_cols] = (grad * dsig[rows, cols]).astype(BF16)
        return carry

    lax.fori_loop(0, COLS, assemble, 0)

    stores = []
    for m in range(2):
        rows = slice(m * 256, m * 256 + 256)
        h = lax.dot_general(d_mixed[rows, :], w_in[...], NT, preferred_element_type=F32)
        h = h * gain
        hat = x_hat[rows, :]
        mean = jnp.mean(h, axis=1, keepdims=True)
        along = jnp.mean(h * hat, axis=1, keepdims=True)
        scale = rstd[rows, 0:1]
        out_buf[rows, :] = (inc[rows, :].astype(F32) + scale * (h - mean - hat * along)).astype(BF16)
        store = pltpu.make_async_copy(
            out_buf.at[pl.ds(m * 256, 256)], out_hbm.at[pl.ds(m * 256, 256)], out_sem.at[m]
        )
        store.start()
        stores.append(store)

    settle(0)
    wait_bytes(ids_line.at[pl.ds(0, NZ - 1)], ids_send.at[0])
    wait_bytes(ids_all.at[pl.ds(0, 7)], ids_send.at[1])
    edges_out(enc, EDGE, 0)
    edges_out(d_pre, PAD, 1)
    sum_done(0)
    sum_done(1)
    for store in stores:
        store.wait()


def local(
    enc_input,
    llm_grads,
    slot_block,
    utt_lengths,
    ln_gain,
    ln_bias,
    w_in,
    dw_kernel,
    bn_gain,
    bn_bias,
    w_out,
):
    vmem = pl.BlockSpec(memory_space=pltpu.VMEM)
    hbm = pl.BlockSpec(memory_space=pl.ANY)
    dma = pltpu.SemaphoreType.DMA
    full = pltpu.VMEM((FRAMES, C), F32)
    wide = pltpu.VMEM((EXT, C), F32)
    blocks = pltpu.VMEM((SHARDS, BLK, C), BF16)
    out = pl.pallas_call(
        kernel,
        out_shape=jax.ShapeDtypeStruct((FRAMES, C), BF16),
        in_specs=[hbm] * 4 + [vmem] * 7,
        out_specs=hbm,
        scratch_shapes=[
            pltpu.VMEM((WIDE, C), BF16),
            blocks,
            pltpu.VMEM((C, 2 * C), BF16),
            pltpu.VMEM((C, C), BF16),
            blocks,
            blocks,
            pltpu.VMEM((8, LANES), I32),
            pltpu.SMEM((1, LANES), I32),
            pltpu.SMEM((1, LANES), I32),
            pltpu.VMEM((NZ, 1, LANES), I32),
            pltpu.VMEM((NZ, LANES), I32),
            pltpu.VMEM((8, NZ, LANES), I32),
            pltpu.VMEM((8, UTT_PAD), I32),
            pltpu.VMEM((WIDE, LANES), F32),
            pltpu.VMEM((TAPS, EXT, LANES), F32),
            full,
            pltpu.VMEM((FRAMES, LANES), F32),
            pltpu.VMEM((WIDE, C), BF16),
            full,
            full,
            pltpu.VMEM((WIDE, C), F32),
            wide,
            full,
            full,
            full,
            full,
            wide,
            pltpu.VMEM((FRAMES, C), BF16),
            pltpu.VMEM((FRAMES, 2 * C), BF16),
            pltpu.VMEM((FRAMES, C), BF16),
            pltpu.VMEM((2, 4, 2, COLS, LANES), F32),
            pltpu.VMEM((2, 1, 2, COLS, LANES), F32),
            pltpu.VMEM((2, 15, 2, COLS, LANES), F32),
            pltpu.VMEM((2, 7, 2, COLS, LANES), F32),
            dma((4,)),
            dma((2,)),
            dma((WIN,)),
            dma,
            dma((2,)),
            dma((2,)),
            dma((2, 2)),
            dma((2, 2)),
            dma((2, 3)),
            dma((2, 3)),
            dma((2,)),
            pltpu.SemaphoreType.REGULAR,
        ],
        compiler_params=pltpu.CompilerParams(
            collective_id=1, has_side_effects=True, vmem_limit_bytes=56 << 20
        ),
        name="conv_module_back",
    )(
        enc_input[0],
        llm_grads[0].reshape(SHARDS, BLK, C),
        w_in,
        w_out,
        slot_block,
        utt_lengths,
        ln_gain.reshape(1, C),
        ln_bias.reshape(1, C),
        dw_kernel,
        bn_gain.reshape(COLS, LANES),
        bn_bias.reshape(COLS, LANES),
    )
    return out[None]


def solution(mesh):
    in_specs = (
        P("dp", ("sec", "tm"), None),
        P("dp", ("sec", "tm"), None),
        P("dp", ("sec", "tm")),
        P("dp", None),
        P(),
        P(),
        P(),
        P(),
        P(),
        P(),
        P(),
    )
    out_specs = P("dp", ("sec", "tm"), None)
    return jax.shard_map(local, mesh=mesh, in_specs=in_specs, out_specs=out_specs, check_vma=False)
```

```python
import functools

import jax
import jax.numpy as jnp
from jax import lax
from jax.experimental import pallas as pl
from jax.experimental.pallas import tpu as pltpu
from jax.sharding import PartitionSpec as P

MESH = pl.DeviceIdType.MESH
F32 = jnp.float32
BF16 = jnp.bfloat16
I32 = jnp.int32

EPS = 1e-05
SEC, NZ, NY, NX = 2, 8, 4, 4
SHARDS = SEC * NZ * NY
FRAMES = 512
C = 1024
TAPS = 9
HALF = 4
PAD = 8
EXT = FRAMES + 2 * PAD
EDGE = 16
THIRD = EXT // 3
WIDE = FRAMES + 2 * EDGE
BLK = 16
NBE = 32
UTT = 262
UTT_PAD = 384
LANES = 128
COLS = C // LANES
ROWS = 128
WIN = 20
SENDS = SHARDS - 1
ALL_FRAMES = float(FRAMES * SHARDS * NX)
NT = (((1,), (1,)), ((), ()))


def wrap(value, count):
    return lax.rem(value + count, count)


def kernel(
    enc_hbm,
    llm_hbm,
    w_in_hbm,
    w_out_hbm,
    slot_ref,
    utt_ref,
    ln_gain_ref,
    ln_bias_ref,
    dw_ref,
    bn_gain_ref,
    bn_bias_ref,
    out_ref,
    enc,
    llm,
    w_in,
    w_out,
    send,
    recv,
    row_buf,
    slot_tbl,
    src_tbl,
    ids_line,
    ids_tile,
    ids_all,
    utt_pad,
    seg,
    masks,
    x_hat,
    rstd,
    normed,
    sig,
    dsig,
    gated,
    conv,
    swish,
    ones_t,
    z_t,
    d_t,
    d_pre,
    inc,
    d_mixed,
    ar_src,
    ar_s,
    ar_xy,
    ar_z,
    load_sem,
    tbl_sem,
    a2a_send,
    a2a_recv,
    ids_send,
    ids_recv,
    halo_send,
    halo_recv,
    ar_send,
    ar_recv,
    lines_in,
):
    sec = lax.axis_index("sec")
    tm = lax.axis_index("tm")
    dp = lax.axis_index("dp")
    z = tm // NY
    y = lax.rem(tm, NY)
    me = sec * (NZ * NY) + tm

    def place(s_at, z_at, y_at, x_at):
        return {"sec": s_at, "tm": z_at * NY + y_at, "dp": x_at}

    loads = []
    for k, (source, target) in enumerate(
        ((llm_hbm, llm), (enc_hbm, enc.at[pl.ds(EDGE, FRAMES)]), (w_in_hbm, w_in), (w_out_hbm, w_out))
    ):
        load = pltpu.make_async_copy(source, target, load_sem.at[k])
        load.start()
        loads.append(load)

    def partner(i):
        k = lax.rem(i, NZ)
        q = 7 - i // NZ
        dz = 4 + ((k + 1) // 2) * (1 - 2 * lax.rem(k, 2))
        return (
            lax.rem(sec + lax.rem(q, 2), SEC),
            lax.rem(z + dz, NZ),
            lax.rem(y + q // 2, NY),
        )

    line = [(sec, wrap(z + d, NZ), y, dp) for d in (4, 3, 5, 2, 6, 1, 7)]
    cross = [
        (sec, z, wrap(y + j, NY), wrap(dp + i, NX))
        for j in (2, 1, 3, 0)
        for i in (2, 1, 3, 0)
        if (i, j) != (0, 0)
    ]
    mate = [(1 - sec, z, y, dp)]
    plane = [
        (wrap(sec + s, SEC), z, wrap(y + j, NY), dp)
        for j in (2, 1, 3, 0)
        for s in (1, 0)
        if (s, j) != (0, 0)
    ]

    barrier = pltpu.get_barrier_semaphore()
    x_line = [(sec, z, y, wrap(dp + i, NX)) for i in (2, 1, 3)]
    greeted = line + plane + x_line
    for p in greeted:
        pl.semaphore_signal(barrier, inc=1, device_id=place(*p), device_id_type=MESH)

    slot_row = slot_ref[...]
    lane = lax.broadcasted_iota(I32, (64, LANES), 1)
    sub = lax.broadcasted_iota(I32, (64, LANES), 0)
    lane64 = lax.broadcasted_iota(I32, (64, 64), 1)
    sub64 = lax.broadcasted_iota(I32, (64, 64), 0)
    slot_col = jnp.sum(
        jnp.where(lane64 == sub64, jnp.broadcast_to(slot_row, (64, 64)), 0), axis=1, keepdims=True
    )
    hit = (slot_col >= lane * NBE) & (slot_col < lane * NBE + NBE)
    row_buf[0:1, :] = jnp.sum(jnp.where(hit, sub, 0), axis=0, keepdims=True)
    ids_row = jnp.sum(jnp.where(hit, slot_col + 1, 0), axis=0, keepdims=True) - 1
    tbl = pltpu.make_async_copy(row_buf.at[pl.ds(0, 1)], slot_tbl, tbl_sem.at[0])
    tbl.start()
    ids_line[z] = ids_row
    loads[0].wait()
    tbl.wait()

    def pack(d, carry):
        send[d] = llm[jnp.clip(slot_tbl[0, d], 0, 63)]
        return carry

    lax.fori_loop(0, SHARDS, pack, 0)
    recv[me] = send[me]

    pl.semaphore_wait(barrier, len(greeted))
    for p in plane:
        pl.semaphore_signal(lines_in, inc=1, device_id=place(*p), device_id_type=MESH)
    pl.semaphore_wait(lines_in, len(plane))

    def spread(partners, source, target_of, s_sem, r_sem):
        for i, p in enumerate(partners):
            pltpu.make_async_remote_copy(
                source, target_of(i), s_sem, r_sem, device_id=place(*p), device_id_type=MESH
            ).start()

    def wait_bytes(ref, sem):
        pltpu.make_async_copy(ref, ref, sem).wait()

    before = wrap(me + SHARDS - 1, SHARDS)
    after = wrap(me + 1, SHARDS)

    def edges(buf, rows, k):
        for j, (to, start, end) in enumerate(
            ((after, FRAMES, 0), (before, rows, rows + FRAMES))
        ):
            pltpu.make_async_remote_copy(
                buf.at[pl.ds(start, rows)],
                buf.at[pl.ds(end, rows)],
                halo_send.at[k, j],
                halo_recv.at[k, j],
                device_id={"sec": to // (NZ * NY), "tm": lax.rem(to, NZ * NY), "dp": dp},
                device_id_type=MESH,
            ).start()

    def edges_in(buf, rows, k):
        wait_bytes(buf.at[pl.ds(0, rows)], halo_recv.at[k, 0])
        wait_bytes(buf.at[pl.ds(0, rows)], halo_recv.at[k, 1])

    def edges_out(buf, rows, k):
        wait_bytes(buf.at[pl.ds(0, rows)], halo_send.at[k, 0])
        wait_bytes(buf.at[pl.ds(0, rows)], halo_send.at[k, 1])

    loads[1].wait()
    edges(enc, EDGE, 0)
    spread(line, ids_line.at[z], lambda i: ids_line.at[z], ids_send.at[0], ids_recv.at[0])

    def block_copy(i):
        s_at, z_at, y_at = partner(i)
        to = s_at * (NZ * NY) + z_at * NY + y_at
        return pltpu.make_async_remote_copy(
            send.at[to],
            recv.at[me],
            a2a_send.at[lax.rem(i, WIN)],
            a2a_recv,
            device_id=place(s_at, z_at, y_at, dp),
            device_id_type=MESH,
        )

    started = [0]
    ended = [0]

    def begin(count):
        low, high = started[0], min(SENDS, started[0] + count)
        started[0] = high
        assert high - ended[0] <= WIN

        def step(i, carry):
            block_copy(i).start()
            return carry

        if high > low:
            lax.fori_loop(low, high, step, 0)

    def settle(left):
        low, high = ended[0], max(ended[0], started[0] - left)
        ended[0] = high

        def step(i, carry):
            block_copy(i).wait_send()
            return carry

        if high > low:
            lax.fori_loop(low, high, step, 0)

    def reserve(count):
        first = (ended[0], started[0])
        ended[0] += count
        started[0] += count
        assert started[0] <= SENDS
        return first

    def pump(first, i):
        block_copy(first[0] + i).wait_send()
        block_copy(first[1] + i).start()

    begin(6)

    gain = ln_gain_ref[...]
    bias = ln_bias_ref[...]

    def norm_rows(values):
        values = values.astype(F32)
        mean = jnp.mean(values, axis=1, keepdims=True)
        centred = values - mean
        scale = lax.rsqrt(jnp.mean(centred * centred, axis=1, keepdims=True) + EPS)
        hat = centred * scale
        return hat, scale, (hat * gain + bias).astype(BF16)

    def norm(r, carry):
        rows = pl.ds(pl.multiple_of(r * 64, 64), 64)
        wide_rows = pl.ds(pl.multiple_of(r * 64 + EDGE, EDGE), 64)
        hat, scale, out = norm_rows(enc[wide_rows, :])
        rstd[rows, :] = jnp.broadcast_to(scale, (64, LANES))
        x_hat[rows, :] = hat
        normed[wide_rows, :] = out
        return carry

    lax.fori_loop(0, 8, norm, 0)

    utt_pad[...] = jnp.zeros((8, UTT_PAD), I32)
    utt_pad[0:1, 0:UTT] = utt_ref[...]
    lengths = utt_pad[...].astype(F32).astype(BF16)
    upper = (
        lax.broadcasted_iota(I32, (UTT_PAD, UTT_PAD), 0)
        <= lax.broadcasted_iota(I32, (UTT_PAD, UTT_PAD), 1)
    ).astype(F32).astype(BF16)
    ends = jnp.dot(lengths, upper, preferred_element_type=F32)[0:1, :]

    def number(r, carry):
        rows = pl.ds(pl.multiple_of(r * 136, 8), 136)
        position = lax.broadcasted_iota(I32, (136, 1), 0) + (r * 136 + me * FRAMES - EDGE)
        position_f = position.astype(F32)
        count = jnp.sum((position_f >= ends).astype(F32), axis=1, keepdims=True)
        inside = (position >= 0) & (position < SHARDS * FRAMES)
        seg[rows, :] = jnp.broadcast_to(jnp.where(inside, count, -1.0), (136, LANES))
        return carry

    lax.fori_loop(0, WIDE // 136, number, 0)

    def mark(r, carry):
        window = seg[pl.ds(pl.multiple_of(r * THIRD, 16), THIRD + 2 * PAD), :]
        own = window[PAD : PAD + THIRD]
        rows = pl.ds(pl.multiple_of(r * THIRD, 16), THIRD)
        for j in range(TAPS):
            masks[j, rows, :] = (window[HALF + j : HALF + j + THIRD] == own).astype(F32)
        return carry

    lax.fori_loop(0, EXT // THIRD, mark, 0)

    edges_in(enc, EDGE, 0)
    for start in (0, EDGE + FRAMES):
        normed[start : start + EDGE, :] = norm_rows(enc[start : start + EDGE, :])[2]

    loads[2].wait()
    moved = reserve(4)

    def project(n, carry):
        at = pl.ds(pl.multiple_of(n * 256, 256), 256)
        gate_at = pl.ds(pl.multiple_of(C + n * 256, 256), 256)
        lin = jnp.dot(normed[...], w_in[:, at], preferred_element_type=F32)
        gate = jnp.dot(normed[...], w_in[:, gate_at], preferred_element_type=F32)
        pump(moved, n)
        s = jax.nn.sigmoid(gate)
        mixed = lin * s
        sig[:, at] = s[EDGE : EDGE + FRAMES]
        dsig[:, at] = (mixed * (1.0 - s))[EDGE : EDGE + FRAMES]
        gated[:, at] = mixed.astype(BF16).astype(F32)
        return carry

    lax.fori_loop(0, 4, project, 0)

    moved_conv = reserve(4)

    def convolve(c, carry):
        cols = pl.ds(pl.multiple_of(c * LANES, LANES), LANES)
        taps = dw_ref[:, cols]
        first_sum = jnp.zeros((1, LANES), F32)
        second_sum = jnp.zeros((1, LANES), F32)
        for r in range(EXT // THIRD):
            window = gated[r * THIRD : r * THIRD + THIRD + 2 * PAD, cols]
            total = jnp.zeros((THIRD, LANES), F32)
            for k in range(TAPS):
                part = window[HALF + k : HALF + k + THIRD]
                if k != HALF:
                    part = part * masks[k, r * THIRD : r * THIRD + THIRD, :]
                total = total + taps[k : k + 1, :] * part
            conv[r * THIRD : r * THIRD + THIRD, cols] = total
            own = total[(PAD if r == 0 else 0) : (THIRD - PAD if r == EXT // THIRD - 1 else THIRD)]
            first_sum = first_sum + jnp.sum(own, axis=0, keepdims=True)
            second_sum = second_sum + jnp.sum(own * own, axis=0, keepdims=True)
        ar_src[0, 0, 0, pl.ds(c, 1), :] = first_sum
        ar_src[0, 0, 1, pl.ds(c, 1), :] = second_sum

        @pl.when(lax.rem(c, 2) == 0)
        def _():
            pump(moved_conv, c // 2)

        return carry

    lax.fori_loop(0, COLS, convolve, 0)

    groups = ((mate, ar_s), (cross, ar_xy), (line, ar_z))

    def sum_send(k, step):
        partners, target = groups[step]
        spread(
            partners,
            ar_src.at[k, step],
            lambda i: target.at[k, i],
            ar_send.at[k, step],
            ar_recv.at[k, step],
        )

    def sum_recv(k, step):
        partners, target = groups[step]
        count = len(partners)
        wait_bytes(target.at[k, pl.ds(0, count)], ar_recv.at[k, step])
        total = ar_src[k, step]
        for i in range(count):
            total = total + target[k, i]
        ar_src[k, step + 1] = total

    def sum_done(k):
        for step, (partners, target) in enumerate(groups):
            wait_bytes(target.at[k, pl.ds(0, len(partners))], ar_send.at[k, step])

    settle(4)
    sum_send(0, 0)
    begin(7)

    wait_bytes(ids_line.at[pl.ds(0, NZ - 1)], ids_recv.at[0])
    for j in range(NZ):
        ids_tile[j : j + 1, :] = ids_line[j]
    here = sec * NY + y
    ids_all[here] = ids_tile[...]
    spread(plane, ids_tile, lambda i: ids_all.at[here], ids_send.at[1], ids_recv.at[1])

    sum_recv(0, 0)
    settle(3)
    sum_send(0, 1)
    begin(14)
    sum_recv(0, 1)
    settle(3)
    sum_send(0, 2)
    begin(14)
    sum_recv(0, 2)

    wait_bytes(ids_all.at[pl.ds(0, 7)], ids_recv.at[1])
    ids = ids_all[...].reshape(64, LANES)
    mine = jnp.sum(jnp.where(lane == me, ids, 0), axis=1, keepdims=True) - me * NBE
    quarter = sub // NZ
    source = (quarter // NY) * (NZ * NY) + lax.rem(sub, NZ) * NY + lax.rem(quarter, NY)
    row_buf[1:2, :] = jnp.sum(jnp.where(mine == lane, source, 0), axis=0, keepdims=True)
    src_copy = pltpu.make_async_copy(row_buf.at[pl.ds(1, 1)], src_tbl, tbl_sem.at[1])
    src_copy.start()

    moved_bn = reserve(8)

    def bn_scales(c):
        bn_mean = ar_src[0, 3, 0, pl.ds(c, 1), :] / ALL_FRAMES
        bn_var = ar_src[0, 3, 1, pl.ds(c, 1), :] / ALL_FRAMES - bn_mean * bn_mean
        return bn_mean, lax.rsqrt(bn_var + EPS)

    def normalise(c, carry):
        cols = pl.ds(pl.multiple_of(c * LANES, LANES), LANES)
        bn_mean, bn_rstd = bn_scales(c)
        bn_gain = bn_gain_ref[pl.ds(c, 1), :]
        bn_bias = bn_bias_ref[pl.ds(c, 1), :]
        taps = dw_ref[:, cols]
        factor = bn_gain * bn_rstd
        for r in range(EXT // 48):
            rows = slice(r * 48, r * 48 + 48)
            conv[rows, cols] = (conv[rows, cols] - bn_mean) * bn_rstd
        for r in range(FRAMES // ROWS):
            rows = slice(r * ROWS, r * ROWS + ROWS)
            window = conv[r * ROWS : r * ROWS + ROWS + 2 * PAD, cols]
            pre = window[PAD : PAD + ROWS] * bn_gain + bn_bias
            s = jax.nn.sigmoid(pre)
            swish[rows, cols] = s * (1.0 + pre * (1.0 - s))
            ones_total = jnp.zeros((ROWS, LANES), F32)
            z_total = jnp.zeros((ROWS, LANES), F32)
            for j in range(TAPS):
                weight = (taps[TAPS - 1 - j : TAPS - j, :] * factor) * masks[j, PAD + r * ROWS : PAD + r * ROWS + ROWS, :]
                ones_total = ones_total + weight
                z_total = z_total + weight * window[HALF + j : HALF + j + ROWS]
            ones_t[rows, cols] = ones_total
            z_t[rows, cols] = z_total
        pump(moved_bn, c)
        return carry

    lax.fori_loop(0, COLS, normalise, 0)
    src_copy.wait()
    loads[3].wait()
    settle(max(0, WIN - (SENDS - started[0])))
    begin(SENDS)
    assert started[0] == SENDS

    wait_bytes(recv.at[pl.ds(0, SENDS)], a2a_recv)

    def gather(b, carry):
        inc[pl.ds(pl.multiple_of(b * BLK, BLK), BLK), :] = recv[jnp.clip(src_tbl[0, b], 0, 63)]
        return carry

    lax.fori_loop(0, NBE, gather, 0)

    for n in range(4):
        at = slice(n * 256, n * 256 + 256)
        grad = lax.dot_general(inc[...], w_out[at, :], NT, preferred_element_type=F32)
        grad = grad * swish[:, at]
        d_pre[PAD : PAD + FRAMES, at] = grad
        first_sum = jnp.sum(grad, axis=0, keepdims=True)
        cross_sum = jnp.sum(grad * conv[PAD : PAD + FRAMES, at], axis=0, keepdims=True)
        for j in range(2):
            c = 2 * n + j
            ar_src[1, 0, 0, c : c + 1, :] = first_sum[:, j * LANES : (j + 1) * LANES]
            ar_src[1, 0, 1, c : c + 1, :] = cross_sum[:, j * LANES : (j + 1) * LANES]

    def conv_back(c, carry):
        cols = pl.ds(pl.multiple_of(c * LANES, LANES), LANES)
        bn_mean, bn_rstd = bn_scales(c)
        factor = bn_gain_ref[pl.ds(c, 1), :] * bn_rstd
        taps = dw_ref[:, cols] * factor
        for r in range(FRAMES // ROWS):
            rows = slice(r * ROWS, r * ROWS + ROWS)
            window = d_pre[r * ROWS : r * ROWS + ROWS + 2 * PAD, cols]
            total = jnp.zeros((ROWS, LANES), F32)
            for j in range(TAPS):
                part = window[HALF + j : HALF + j + ROWS]
                if j != HALF:
                    part = part * masks[j, PAD + r * ROWS : PAD + r * ROWS + ROWS, :]
                total = total + taps[TAPS - 1 - j : TAPS - j, :] * part
            d_t[rows, cols] = total
        return carry

    sum_send(1, 0)
    edges(d_pre, PAD, 1)
    sum_recv(1, 0)
    sum_send(1, 1)
    edges_in(d_pre, PAD, 1)
    lax.fori_loop(0, COLS // 2, conv_back, 0)
    settle(0)
    wait_bytes(ids_line.at[pl.ds(0, NZ - 1)], ids_send.at[0])
    wait_bytes(ids_all.at[pl.ds(0, 7)], ids_send.at[1])
    edges_out(enc, EDGE, 0)
    sum_done(0)
    sum_recv(1, 1)
    sum_send(1, 2)
    lax.fori_loop(COLS // 2, COLS, conv_back, 0)
    sum_recv(1, 2)

    def assemble(c, carry):
        cols = pl.ds(pl.multiple_of(c * LANES, LANES), LANES)
        gate_cols = pl.ds(pl.multiple_of(C + c * LANES, LANES), LANES)
        grad_mean = ar_src[1, 3, 0, pl.ds(c, 1), :] / ALL_FRAMES
        cross_mean = ar_src[1, 3, 1, pl.ds(c, 1), :] / ALL_FRAMES
        for r in range(FRAMES // ROWS):
            rows = slice(r * ROWS, r * ROWS + ROWS)
            grad = d_t[rows, cols] - grad_mean * ones_t[rows, cols] - cross_mean * z_t[rows, cols]
            d_mixed[rows, cols] = (grad * sig[rows, cols]).astype(BF16)
            d_mixed[rows, gate_cols] = (grad * dsig[rows, cols]).astype(BF16)
        return carry

    lax.fori_loop(0, COLS, assemble, 0)

    for m in range(2):
        rows = slice(m * 256, m * 256 + 256)
        h = lax.dot_general(d_mixed[rows, :], w_in[...], NT, preferred_element_type=F32)
        h = h * gain
        hat = x_hat[rows, :]
        mean = jnp.mean(h, axis=1, keepdims=True)
        along = jnp.mean(h * hat, axis=1, keepdims=True)
        scale = rstd[rows, 0:1]
        out_ref[rows, :] = (inc[rows, :].astype(F32) + scale * (h - mean - hat * along)).astype(BF16)

    edges_out(d_pre, PAD, 1)
    sum_done(1)


def local(
    enc_input,
    llm_grads,
    slot_block,
    utt_lengths,
    ln_gain,
    ln_bias,
    w_in,
    dw_kernel,
    bn_gain,
    bn_bias,
    w_out,
):
    vmem = pl.BlockSpec(memory_space=pltpu.VMEM)
    hbm = pl.BlockSpec(memory_space=pltpu.HBM)
    dma = pltpu.SemaphoreType.DMA
    full = pltpu.VMEM((FRAMES, C), F32)
    wide = pltpu.VMEM((EXT, C), F32)
    blocks = pltpu.VMEM((SHARDS, BLK, C), BF16)
    out = pl.pallas_call(
        kernel,
        out_shape=jax.ShapeDtypeStruct((FRAMES, C), BF16),
        in_specs=[hbm] * 4 + [vmem] * 7,
        out_specs=vmem,
        scratch_shapes=[
            pltpu.VMEM((WIDE, C), BF16),
            blocks,
            pltpu.VMEM((C, 2 * C), BF16),
            pltpu.VMEM((C, C), BF16),
            blocks,
            blocks,
            pltpu.VMEM((8, LANES), I32),
            pltpu.SMEM((1, LANES), I32),
            pltpu.SMEM((1, LANES), I32),
            pltpu.VMEM((NZ, 1, LANES), I32),
            pltpu.VMEM((NZ, LANES), I32),
            pltpu.VMEM((8, NZ, LANES), I32),
            pltpu.VMEM((8, UTT_PAD), I32),
            pltpu.VMEM((WIDE, LANES), F32),
            pltpu.VMEM((TAPS, EXT, LANES), F32),
            full,
            pltpu.VMEM((FRAMES, LANES), F32),
            pltpu.VMEM((WIDE, C), BF16),
            full,
            full,
            pltpu.VMEM((WIDE, C), F32),
            wide,
            full,
            full,
            full,
            full,
            wide,
            pltpu.VMEM((FRAMES, C), BF16),
            pltpu.VMEM((FRAMES, 2 * C), BF16),
            pltpu.VMEM((2, 4, 2, COLS, LANES), F32),
            pltpu.VMEM((2, 1, 2, COLS, LANES), F32),
            pltpu.VMEM((2, 15, 2, COLS, LANES), F32),
            pltpu.VMEM((2, 7, 2, COLS, LANES), F32),
            dma((4,)),
            dma((2,)),
            dma((WIN,)),
            dma,
            dma((2,)),
            dma((2,)),
            dma((2, 2)),
            dma((2, 2)),
            dma((2, 3)),
            dma((2, 3)),
            pltpu.SemaphoreType.REGULAR,
        ],
        compiler_params=pltpu.CompilerParams(
            collective_id=1, has_side_effects=True, vmem_limit_bytes=52 << 20
        ),
        name="conv_module_back",
    )(
        enc_input[0],
        llm_grads[0].reshape(SHARDS, BLK, C),
        w_in,
        w_out,
        slot_block,
        utt_lengths,
        ln_gain.reshape(1, C),
        ln_bias.reshape(1, C),
        dw_kernel,
        bn_gain.reshape(COLS, LANES),
        bn_bias.reshape(COLS, LANES),
    )
    return out[None]


def solution(mesh):
    in_specs = (
        P("dp", ("sec", "tm"), None),
        P("dp", ("sec", "tm"), None),
        P("dp", ("sec", "tm")),
        P("dp", None),
        P(),
        P(),
        P(),
        P(),
        P(),
        P(),
        P(),
    )
    out_specs = P("dp", ("sec", "tm"), None)
    return jax.shard_map(local, mesh=mesh, in_specs=in_specs, out_specs=out_specs, check_vma=False)
```

```python
import functools

import jax
import jax.numpy as jnp
from jax import lax
from jax.experimental import pallas as pl
from jax.experimental.pallas import tpu as pltpu
from jax.sharding import PartitionSpec as P

FIRST = 6
MESH = pl.DeviceIdType.MESH
F32 = jnp.float32
BF16 = jnp.bfloat16
I32 = jnp.int32

EPS = 1e-05
SEC, NZ, NY, NX = 2, 8, 4, 4
SHARDS = SEC * NZ * NY
FRAMES = 512
C = 1024
TAPS = 9
HALF = 4
PAD = 8
EXT = FRAMES + 2 * PAD
EDGE = 16
THIRD = EXT // 3
WIDE = FRAMES + 2 * EDGE
BLK = 16
NBE = 32
UTT = 262
UTT_PAD = 384
LANES = 128
COLS = C // LANES
ROWS = 128
SENDS = SHARDS - 1
ALL_FRAMES = float(FRAMES * SHARDS * NX)
NT = (((1,), (1,)), ((), ()))


def wrap(value, count):
    return lax.rem(value + count, count)


def kernel(
    enc_hbm,
    llm_hbm,
    w_in_hbm,
    w_out_hbm,
    slot_ref,
    utt_ref,
    ln_gain_ref,
    ln_bias_ref,
    dw_ref,
    bn_gain_ref,
    bn_bias_ref,
    out_hbm,
    enc,
    llm,
    w_in,
    w_out,
    send,
    recv,
    row_buf,
    slot_tbl,
    src_tbl,
    ids_line,
    ids_tile,
    ids_all,
    utt_pad,
    seg,
    masks,
    x_hat,
    rstd,
    normed,
    sig,
    dsig,
    gated,
    conv,
    swish,
    ones_t,
    z_t,
    d_t,
    d_pre,
    inc,
    d_mixed,
    out_buf,
    ar_src,
    ar_s,
    ar_xy,
    ar_z,
    load_sem,
    tbl_sem,
    a2a_send,
    a2a_recv,
    ids_send,
    ids_recv,
    halo_send,
    halo_recv,
    ar_send,
    ar_recv,
    out_sem,
    lines_in,
):
    sec = lax.axis_index("sec")
    tm = lax.axis_index("tm")
    dp = lax.axis_index("dp")
    z = tm // NY
    y = lax.rem(tm, NY)
    me = sec * (NZ * NY) + tm

    def place(s_at, z_at, y_at, x_at):
        return {"sec": s_at, "tm": z_at * NY + y_at, "dp": x_at}

    loads = []
    for k, (source, target) in enumerate(
        ((llm_hbm, llm), (enc_hbm, enc.at[pl.ds(EDGE, FRAMES)]), (w_in_hbm, w_in), (w_out_hbm, w_out))
    ):
        load = pltpu.make_async_copy(source, target, load_sem.at[k])
        load.start()
        loads.append(load)

    def partner(i):
        k = lax.rem(i, NZ)
        q = 7 - i // NZ
        dz = 4 + ((k + 1) // 2) * (1 - 2 * lax.rem(k, 2))
        return (
            lax.rem(sec + lax.rem(q, 2), SEC),
            lax.rem(z + dz, NZ),
            lax.rem(y + q // 2, NY),
        )

    line = [(sec, wrap(z + d, NZ), y, dp) for d in (4, 3, 5, 2, 6, 1, 7)]
    cross = [
        (sec, z, wrap(y + j, NY), wrap(dp + i, NX))
        for j in (2, 1, 3, 0)
        for i in (2, 1, 3, 0)
        if (i, j) != (0, 0)
    ]
    mate = [(1 - sec, z, y, dp)]
    plane = [
        (wrap(sec + s, SEC), z, wrap(y + j, NY), dp)
        for j in (2, 1, 3, 0)
        for s in (1, 0)
        if (s, j) != (0, 0)
    ]

    barrier = pltpu.get_barrier_semaphore()
    x_line = [(sec, z, y, wrap(dp + i, NX)) for i in (2, 1, 3)]
    greeted = line + plane + x_line
    for p in greeted:
        pl.semaphore_signal(barrier, inc=1, device_id=place(*p), device_id_type=MESH)

    slot_row = slot_ref[...]
    lane = lax.broadcasted_iota(I32, (64, LANES), 1)
    sub = lax.broadcasted_iota(I32, (64, LANES), 0)
    lane64 = lax.broadcasted_iota(I32, (64, 64), 1)
    sub64 = lax.broadcasted_iota(I32, (64, 64), 0)
    slot_col = jnp.sum(
        jnp.where(lane64 == sub64, jnp.broadcast_to(slot_row, (64, 64)), 0), axis=1, keepdims=True
    )
    hit = (slot_col >= lane * NBE) & (slot_col < lane * NBE + NBE)
    row_buf[0:1, :] = jnp.sum(jnp.where(hit, sub, 0), axis=0, keepdims=True)
    ids_row = jnp.sum(jnp.where(hit, slot_col + 1, 0), axis=0, keepdims=True) - 1
    tbl = pltpu.make_async_copy(row_buf.at[pl.ds(0, 1)], slot_tbl, tbl_sem.at[0])
    tbl.start()
    ids_line[z] = ids_row

    pl.semaphore_wait(barrier, len(greeted))
    for p in plane:
        pl.semaphore_signal(lines_in, inc=1, device_id=place(*p), device_id_type=MESH)
    loads[0].wait()
    tbl.wait()

    def pack_to(to):
        send[to] = llm[jnp.clip(slot_tbl[0, to], 0, 63)]

    def pack(i):
        s_at, z_at, y_at = partner(i)
        pack_to(s_at * (NZ * NY) + z_at * NY + y_at)

    for i in range(FIRST):
        pack(i)
    pl.semaphore_wait(lines_in, len(plane))

    def spread(partners, source, target_of, s_sem, r_sem):
        for i, p in enumerate(partners):
            pltpu.make_async_remote_copy(
                source, target_of(i), s_sem, r_sem, device_id=place(*p), device_id_type=MESH
            ).start()

    def wait_bytes(ref, sem):
        pltpu.make_async_copy(ref, ref, sem).wait()

    before = wrap(me + SHARDS - 1, SHARDS)
    after = wrap(me + 1, SHARDS)

    def edges(buf, rows, k):
        for j, (to, start, end) in enumerate(
            ((after, FRAMES, 0), (before, rows, rows + FRAMES))
        ):
            pltpu.make_async_remote_copy(
                buf.at[pl.ds(start, rows)],
                buf.at[pl.ds(end, rows)],
                halo_send.at[k, j],
                halo_recv.at[k, j],
                device_id={"sec": to // (NZ * NY), "tm": lax.rem(to, NZ * NY), "dp": dp},
                device_id_type=MESH,
            ).start()

    def edges_in(buf, rows, k):
        wait_bytes(buf.at[pl.ds(0, rows)], halo_recv.at[k, 0])
        wait_bytes(buf.at[pl.ds(0, rows)], halo_recv.at[k, 1])

    def edges_out(buf, rows, k):
        wait_bytes(buf.at[pl.ds(0, rows)], halo_send.at[k, 0])
        wait_bytes(buf.at[pl.ds(0, rows)], halo_send.at[k, 1])

    loads[1].wait()
    edges(enc, EDGE, 0)
    spread(line, ids_line.at[z], lambda i: ids_line.at[z], ids_send.at[0], ids_recv.at[0])

    def block_copy(i):
        s_at, z_at, y_at = partner(i)
        to = s_at * (NZ * NY) + z_at * NY + y_at
        return pltpu.make_async_remote_copy(
            send.at[to],
            recv.at[me],
            a2a_send.at[i],
            a2a_recv,
            device_id=place(s_at, z_at, y_at, dp),
            device_id_type=MESH,
        )

    started = [0]
    ended = [0]

    def begin(count):
        low, high = started[0], min(SENDS, started[0] + count)
        started[0] = high

        def step(i, carry):
            block_copy(i).start()
            return carry

        if high > low:
            lax.fori_loop(low, high, step, 0)

    def settle(left):
        low, high = ended[0], max(ended[0], started[0] - left)
        ended[0] = high

        def step(i, carry):
            block_copy(i).wait_send()
            return carry

        if high > low:
            lax.fori_loop(low, high, step, 0)

    def reserve(count):
        first = started[0]
        started[0] += count
        assert started[0] <= SENDS
        return first

    def pump(first, i):
        block_copy(first + i).start()

    begin(FIRST)

    def pack_more(i, carry):
        for j in range(3):
            pack(FIRST + 3 * i + j)
        return carry

    lax.fori_loop(0, (SENDS - FIRST) // 3, pack_more, 0)
    recv[me] = llm[jnp.clip(slot_tbl[0, me], 0, 63)]
    begin(10)

    gain = ln_gain_ref[...]
    bias = ln_bias_ref[...]

    def norm_rows(values):
        values = values.astype(F32)
        mean = jnp.mean(values, axis=1, keepdims=True)
        centred = values - mean
        scale = lax.rsqrt(jnp.mean(centred * centred, axis=1, keepdims=True) + EPS)
        hat = centred * scale
        return hat, scale, (hat * gain + bias).astype(BF16)

    def norm(r, carry):
        rows = pl.ds(pl.multiple_of(r * 64, 64), 64)
        wide_rows = pl.ds(pl.multiple_of(r * 64 + EDGE, EDGE), 64)
        hat, scale, out = norm_rows(enc[wide_rows, :])
        rstd[rows, :] = jnp.broadcast_to(scale, (64, LANES))
        x_hat[rows, :] = hat
        normed[wide_rows, :] = out
        return carry

    lax.fori_loop(0, 8, norm, 0)

    utt_pad[...] = jnp.zeros((8, UTT_PAD), I32)
    utt_pad[0:1, 0:UTT] = utt_ref[...]
    lengths = utt_pad[...].astype(F32).astype(BF16)
    upper = (
        lax.broadcasted_iota(I32, (UTT_PAD, UTT_PAD), 0)
        <= lax.broadcasted_iota(I32, (UTT_PAD, UTT_PAD), 1)
    ).astype(F32).astype(BF16)
    ends = jnp.dot(lengths, upper, preferred_element_type=F32)[0:1, :]

    def number(r, carry):
        rows = pl.ds(pl.multiple_of(r * 136, 8), 136)
        position = lax.broadcasted_iota(I32, (136, 1), 0) + (r * 136 + me * FRAMES - EDGE)
        position_f = position.astype(F32)
        count = jnp.sum((position_f >= ends).astype(F32), axis=1, keepdims=True)
        inside = (position >= 0) & (position < SHARDS * FRAMES)
        seg[rows, :] = jnp.broadcast_to(jnp.where(inside, count, -1.0), (136, LANES))
        return carry

    lax.fori_loop(0, WIDE // 136, number, 0)

    def mark(r, carry):
        window = seg[pl.ds(pl.multiple_of(r * THIRD, 16), THIRD + 2 * PAD), :]
        own = window[PAD : PAD + THIRD]
        rows = pl.ds(pl.multiple_of(r * THIRD, 16), THIRD)
        for j in range(TAPS):
            masks[j, rows, :] = (window[HALF + j : HALF + j + THIRD] == own).astype(F32)
        return carry

    lax.fori_loop(0, EXT // THIRD, mark, 0)

    edges_in(enc, EDGE, 0)
    for start in (0, EDGE + FRAMES):
        normed[start : start + EDGE, :] = norm_rows(enc[start : start + EDGE, :])[2]

    loads[2].wait()
    moved = reserve(4)

    def project(n, carry):
        at = pl.ds(pl.multiple_of(n * 256, 256), 256)
        gate_at = pl.ds(pl.multiple_of(C + n * 256, 256), 256)
        lin = jnp.dot(normed[...], w_in[:, at], preferred_element_type=F32)
        gate = jnp.dot(normed[...], w_in[:, gate_at], preferred_element_type=F32)
        pump(moved, n)
        s = jax.nn.sigmoid(gate)
        mixed = lin * s
        sig[:, at] = s[EDGE : EDGE + FRAMES]
        dsig[:, at] = (mixed * (1.0 - s))[EDGE : EDGE + FRAMES]
        gated[:, at] = mixed.astype(BF16).astype(F32)
        return carry

    lax.fori_loop(0, 4, project, 0)

    moved_conv = reserve(4)

    def convolve(c, carry):
        cols = pl.ds(pl.multiple_of(c * LANES, LANES), LANES)
        taps = dw_ref[:, cols]
        first_sum = jnp.zeros((1, LANES), F32)
        second_sum = jnp.zeros((1, LANES), F32)
        for r in range(EXT // THIRD):
            window = gated[r * THIRD : r * THIRD + THIRD + 2 * PAD, cols]
            total = jnp.zeros((THIRD, LANES), F32)
            for k in range(TAPS):
                part = window[HALF + k : HALF + k + THIRD]
                if k != HALF:
                    part = part * masks[k, r * THIRD : r * THIRD + THIRD, :]
                total = total + taps[k : k + 1, :] * part
            conv[r * THIRD : r * THIRD + THIRD, cols] = total
            own = total[(PAD if r == 0 else 0) : (THIRD - PAD if r == EXT // THIRD - 1 else THIRD)]
            first_sum = first_sum + jnp.sum(own, axis=0, keepdims=True)
            second_sum = second_sum + jnp.sum(own * own, axis=0, keepdims=True)
        ar_src[0, 0, 0, pl.ds(c, 1), :] = first_sum
        ar_src[0, 0, 1, pl.ds(c, 1), :] = second_sum

        @pl.when(lax.rem(c, 2) == 0)
        def _():
            pump(moved_conv, c // 2)

        return carry

    lax.fori_loop(0, COLS, convolve, 0)

    groups = ((mate, ar_s), (cross, ar_xy), (line, ar_z))

    def sum_send(k, step):
        partners, target = groups[step]
        spread(
            partners,
            ar_src.at[k, step],
            lambda i: target.at[k, i],
            ar_send.at[k, step],
            ar_recv.at[k, step],
        )

    def sum_recv(k, step):
        partners, target = groups[step]
        count = len(partners)
        wait_bytes(target.at[k, pl.ds(0, count)], ar_recv.at[k, step])
        total = ar_src[k, step]
        for i in range(count):
            total = total + target[k, i]
        ar_src[k, step + 1] = total

    def sum_done(k):
        for step, (partners, target) in enumerate(groups):
            wait_bytes(target.at[k, pl.ds(0, len(partners))], ar_send.at[k, step])

    sum_send(0, 0)
    begin(4)

    wait_bytes(ids_line.at[pl.ds(0, NZ - 1)], ids_recv.at[0])
    for j in range(NZ):
        ids_tile[j : j + 1, :] = ids_line[j]
    here = sec * NY + y
    ids_all[here] = ids_tile[...]
    spread(plane, ids_tile, lambda i: ids_all.at[here], ids_send.at[1], ids_recv.at[1])

    sum_recv(0, 0)
    sum_send(0, 1)
    begin(14)
    sum_recv(0, 1)
    sum_send(0, 2)
    begin(SENDS)
    sum_recv(0, 2)

    wait_bytes(ids_all.at[pl.ds(0, 7)], ids_recv.at[1])
    ids = ids_all[...].reshape(64, LANES)
    mine = jnp.sum(jnp.where(lane == me, ids, 0), axis=1, keepdims=True) - me * NBE
    quarter = sub // NZ
    source = (quarter // NY) * (NZ * NY) + lax.rem(sub, NZ) * NY + lax.rem(quarter, NY)
    row_buf[1:2, :] = jnp.sum(jnp.where(mine == lane, source, 0), axis=0, keepdims=True)
    src_copy = pltpu.make_async_copy(row_buf.at[pl.ds(1, 1)], src_tbl, tbl_sem.at[1])
    src_copy.start()


    def bn_scales(c):
        bn_mean = ar_src[0, 3, 0, pl.ds(c, 1), :] / ALL_FRAMES
        bn_var = ar_src[0, 3, 1, pl.ds(c, 1), :] / ALL_FRAMES - bn_mean * bn_mean
        return bn_mean, lax.rsqrt(bn_var + EPS)

    def normalise(c, carry):
        cols = pl.ds(pl.multiple_of(c * LANES, LANES), LANES)
        bn_mean, bn_rstd = bn_scales(c)
        bn_gain = bn_gain_ref[pl.ds(c, 1), :]
        bn_bias = bn_bias_ref[pl.ds(c, 1), :]
        taps = dw_ref[:, cols]
        factor = bn_gain * bn_rstd
        for r in range(EXT // 48):
            rows = slice(r * 48, r * 48 + 48)
            conv[rows, cols] = (conv[rows, cols] - bn_mean) * bn_rstd
        for r in range(FRAMES // ROWS):
            rows = slice(r * ROWS, r * ROWS + ROWS)
            window = conv[r * ROWS : r * ROWS + ROWS + 2 * PAD, cols]
            pre = window[PAD : PAD + ROWS] * bn_gain + bn_bias
            s = jax.nn.sigmoid(pre)
            swish[rows, cols] = s * (1.0 + pre * (1.0 - s))
            ones_total = jnp.zeros((ROWS, LANES), F32)
            z_total = jnp.zeros((ROWS, LANES), F32)
            for j in range(TAPS):
                weight = (taps[TAPS - 1 - j : TAPS - j, :] * factor) * masks[j, PAD + r * ROWS : PAD + r * ROWS + ROWS, :]
                ones_total = ones_total + weight
                z_total = z_total + weight * window[HALF + j : HALF + j + ROWS]
            ones_t[rows, cols] = ones_total
            z_t[rows, cols] = z_total
        return carry

    lax.fori_loop(0, COLS, normalise, 0)
    src_copy.wait()
    loads[3].wait()
    assert started[0] == SENDS

    settle(8)

    wait_bytes(recv.at[pl.ds(0, SENDS)], a2a_recv)

    def gather(b, carry):
        inc[pl.ds(pl.multiple_of(b * BLK, BLK), BLK), :] = recv[jnp.clip(src_tbl[0, b], 0, 63)]
        return carry

    lax.fori_loop(0, NBE, gather, 0)

    for n in range(4):
        at = slice(n * 256, n * 256 + 256)
        grad = lax.dot_general(inc[...], w_out[at, :], NT, preferred_element_type=F32)
        grad = grad * swish[:, at]
        d_pre[PAD : PAD + FRAMES, at] = grad
        first_sum = jnp.sum(grad, axis=0, keepdims=True)
        cross_sum = jnp.sum(grad * conv[PAD : PAD + FRAMES, at], axis=0, keepdims=True)
        for j in range(2):
            c = 2 * n + j
            ar_src[1, 0, 0, c : c + 1, :] = first_sum[:, j * LANES : (j + 1) * LANES]
            ar_src[1, 0, 1, c : c + 1, :] = cross_sum[:, j * LANES : (j + 1) * LANES]

    def conv_back(c, carry):
        cols = pl.ds(pl.multiple_of(c * LANES, LANES), LANES)
        bn_mean, bn_rstd = bn_scales(c)
        factor = bn_gain_ref[pl.ds(c, 1), :] * bn_rstd
        taps = dw_ref[:, cols] * factor
        for r in range(FRAMES // ROWS):
            rows = slice(r * ROWS, r * ROWS + ROWS)
            window = d_pre[r * ROWS : r * ROWS + ROWS + 2 * PAD, cols]
            total = jnp.zeros((ROWS, LANES), F32)
            for j in range(TAPS):
                part = window[HALF + j : HALF + j + ROWS]
                if j != HALF:
                    part = part * masks[j, PAD + r * ROWS : PAD + r * ROWS + ROWS, :]
                total = total + taps[TAPS - 1 - j : TAPS - j, :] * part
            d_t[rows, cols] = total
        return carry

    sum_send(1, 0)
    edges(d_pre, PAD, 1)
    sum_recv(1, 0)
    sum_send(1, 1)
    edges_in(d_pre, PAD, 1)
    lax.fori_loop(0, COLS // 2, conv_back, 0)
    settle(0)
    wait_bytes(ids_line.at[pl.ds(0, NZ - 1)], ids_send.at[0])
    wait_bytes(ids_all.at[pl.ds(0, 7)], ids_send.at[1])
    edges_out(enc, EDGE, 0)
    sum_done(0)
    sum_recv(1, 1)
    sum_send(1, 2)
    lax.fori_loop(COLS // 2, COLS, conv_back, 0)
    sum_recv(1, 2)

    def assemble(c, carry):
        cols = pl.ds(pl.multiple_of(c * LANES, LANES), LANES)
        gate_cols = pl.ds(pl.multiple_of(C + c * LANES, LANES), LANES)
        grad_mean = ar_src[1, 3, 0, pl.ds(c, 1), :] / ALL_FRAMES
        cross_mean = ar_src[1, 3, 1, pl.ds(c, 1), :] / ALL_FRAMES
        for r in range(FRAMES // ROWS):
            rows = slice(r * ROWS, r * ROWS + ROWS)
            grad = d_t[rows, cols] - grad_mean * ones_t[rows, cols] - cross_mean * z_t[rows, cols]
            d_mixed[rows, cols] = (grad * sig[rows, cols]).astype(BF16)
            d_mixed[rows, gate_cols] = (grad * dsig[rows, cols]).astype(BF16)
        return carry

    lax.fori_loop(0, COLS, assemble, 0)

    stores = []
    for m in range(2):
        part = slice(m * 256, m * 256 + 256)
        h = lax.dot_general(d_mixed[part, :], w_in[...], NT, preferred_element_type=F32) * gain
        hat = x_hat[part, :]
        mean = jnp.mean(h, axis=1, keepdims=True)
        along = jnp.mean(h * hat, axis=1, keepdims=True)
        scale = rstd[part, 0:1]
        out_buf[part, :] = (inc[part, :].astype(F32) + scale * (h - mean - hat * along)).astype(BF16)
        at = pl.ds(m * 256, 256)
        store = pltpu.make_async_copy(out_buf.at[at], out_hbm.at[at], out_sem.at[m])
        store.start()
        stores.append(store)

    edges_out(d_pre, PAD, 1)
    sum_done(1)
    for store in stores:
        store.wait()


def local(
    enc_input,
    llm_grads,
    slot_block,
    utt_lengths,
    ln_gain,
    ln_bias,
    w_in,
    dw_kernel,
    bn_gain,
    bn_bias,
    w_out,
):
    vmem = pl.BlockSpec(memory_space=pltpu.VMEM)
    hbm = pl.BlockSpec(memory_space=pl.ANY)
    dma = pltpu.SemaphoreType.DMA
    full = pltpu.VMEM((FRAMES, C), F32)
    wide = pltpu.VMEM((EXT, C), F32)
    blocks = pltpu.VMEM((SHARDS, BLK, C), BF16)
    out = pl.pallas_call(
        kernel,
        out_shape=jax.ShapeDtypeStruct((FRAMES, C), BF16),
        in_specs=[hbm] * 4 + [vmem] * 7,
        out_specs=hbm,
        scratch_shapes=[
            pltpu.VMEM((WIDE, C), BF16),
            blocks,
            pltpu.VMEM((C, 2 * C), BF16),
            pltpu.VMEM((C, C), BF16),
            blocks,
            blocks,
            pltpu.VMEM((8, LANES), I32),
            pltpu.SMEM((1, LANES), I32),
            pltpu.SMEM((1, LANES), I32),
            pltpu.VMEM((NZ, 1, LANES), I32),
            pltpu.VMEM((NZ, LANES), I32),
            pltpu.VMEM((8, NZ, LANES), I32),
            pltpu.VMEM((8, UTT_PAD), I32),
            pltpu.VMEM((WIDE, LANES), F32),
            pltpu.VMEM((TAPS, EXT, LANES), F32),
            full,
            pltpu.VMEM((FRAMES, LANES), F32),
            pltpu.VMEM((WIDE, C), BF16),
            full,
            full,
            pltpu.VMEM((WIDE, C), F32),
            wide,
            full,
            full,
            full,
            full,
            wide,
            pltpu.VMEM((FRAMES, C), BF16),
            pltpu.VMEM((FRAMES, 2 * C), BF16),
            pltpu.VMEM((FRAMES, C), BF16),
            pltpu.VMEM((2, 4, 2, COLS, LANES), F32),
            pltpu.VMEM((2, 1, 2, COLS, LANES), F32),
            pltpu.VMEM((2, 15, 2, COLS, LANES), F32),
            pltpu.VMEM((2, 7, 2, COLS, LANES), F32),
            dma((4,)),
            dma((2,)),
            dma((SENDS,)),
            dma,
            dma((2,)),
            dma((2,)),
            dma((2, 2)),
            dma((2, 2)),
            dma((2, 3)),
            dma((2, 3)),
            dma((4,)),
            pltpu.SemaphoreType.REGULAR,
        ],
        compiler_params=pltpu.CompilerParams(
            collective_id=1, has_side_effects=True, vmem_limit_bytes=56 << 20
        ),
        name="conv_module_back",
    )(
        enc_input[0],
        llm_grads[0].reshape(SHARDS, BLK, C),
        w_in,
        w_out,
        slot_block,
        utt_lengths,
        ln_gain.reshape(1, C),
        ln_bias.reshape(1, C),
        dw_kernel,
        bn_gain.reshape(COLS, LANES),
        bn_bias.reshape(COLS, LANES),
    )
    return out[None]


def solution(mesh):
    in_specs = (
        P("dp", ("sec", "tm"), None),
        P("dp", ("sec", "tm"), None),
        P("dp", ("sec", "tm")),
        P("dp", None),
        P(),
        P(),
        P(),
        P(),
        P(),
        P(),
        P(),
    )
    out_specs = P("dp", ("sec", "tm"), None)
    return jax.shard_map(local, mesh=mesh, in_specs=in_specs, out_specs=out_specs, check_vma=False)
```

```python
import functools

import jax
import jax.numpy as jnp
from jax import lax
from jax.experimental import pallas as pl
from jax.experimental.pallas import tpu as pltpu
from jax.sharding import PartitionSpec as P

FIRST = 6
SMALL = 16
MESH = pl.DeviceIdType.MESH
F32 = jnp.float32
BF16 = jnp.bfloat16
I32 = jnp.int32

EPS = 1e-05
SEC, NZ, NY, NX = 2, 8, 4, 4
SHARDS = SEC * NZ * NY
FRAMES = 512
C = 1024
TAPS = 9
HALF = 4
PAD = 8
EXT = FRAMES + 2 * PAD
EDGE = 16
THIRD = EXT // 3
WIDE = FRAMES + 2 * EDGE
BLK = 16
NBE = 32
UTT = 262
UTT_PAD = 384
LANES = 128
COLS = C // LANES
ROWS = 128
SENDS = SHARDS - 1
ALL_FRAMES = float(FRAMES * SHARDS * NX)
NT = (((1,), (1,)), ((), ()))


def wrap(value, count):
    return lax.rem(value + count, count)


def kernel(
    enc_hbm,
    llm_hbm,
    w_in_hbm,
    w_out_hbm,
    small,
    ints,
    out_ref,
    enc,
    llm,
    w_in,
    w_out,
    send,
    recv,
    row_buf,
    slot_tbl,
    src_tbl,
    ids_line,
    ids_tile,
    ids_all,
    seg,
    masks,
    x_hat,
    rstd,
    normed,
    sig,
    dsig,
    gated,
    conv,
    swish,
    ones_t,
    z_t,
    d_t,
    d_pre,
    inc,
    d_mixed,
    ar_src,
    ar_s,
    ar_xy,
    ar_z,
    load_sem,
    tbl_sem,
    a2a_send,
    a2a_recv,
    ids_send,
    ids_recv,
    halo_send,
    halo_recv,
    ar_send,
    ar_recv,
    lines_in,
):
    sec = lax.axis_index("sec")
    tm = lax.axis_index("tm")
    dp = lax.axis_index("dp")
    z = tm // NY
    y = lax.rem(tm, NY)
    me = sec * (NZ * NY) + tm

    def place(s_at, z_at, y_at, x_at):
        return {"sec": s_at, "tm": z_at * NY + y_at, "dp": x_at}

    loads = []
    for k, (source, target) in enumerate(
        ((llm_hbm, llm), (enc_hbm, enc.at[pl.ds(EDGE, FRAMES)]), (w_in_hbm, w_in), (w_out_hbm, w_out))
    ):
        load = pltpu.make_async_copy(source, target, load_sem.at[k])
        load.start()
        loads.append(load)

    def partner(i):
        k = lax.rem(i, NZ)
        q = 7 - i // NZ
        dz = 4 + ((k + 1) // 2) * (1 - 2 * lax.rem(k, 2))
        return (
            lax.rem(sec + lax.rem(q, 2), SEC),
            lax.rem(z + dz, NZ),
            lax.rem(y + q // 2, NY),
        )

    line = [(sec, wrap(z + d, NZ), y, dp) for d in (4, 3, 5, 2, 6, 1, 7)]
    cross = [
        (sec, z, wrap(y + j, NY), wrap(dp + i, NX))
        for j in (2, 1, 3, 0)
        for i in (2, 1, 3, 0)
        if (i, j) != (0, 0)
    ]
    mate = [(1 - sec, z, y, dp)]
    plane = [
        (wrap(sec + s, SEC), z, wrap(y + j, NY), dp)
        for j in (2, 1, 3, 0)
        for s in (1, 0)
        if (s, j) != (0, 0)
    ]

    barrier = pltpu.get_barrier_semaphore()
    x_line = [(sec, z, y, wrap(dp + i, NX)) for i in (2, 1, 3)]
    greeted = line + plane + x_line
    for p in greeted:
        pl.semaphore_signal(barrier, inc=1, device_id=place(*p), device_id_type=MESH)

    slot_row = ints[:, UTT_PAD : UTT_PAD + 64]
    lane = lax.broadcasted_iota(I32, (64, LANES), 1)
    sub = lax.broadcasted_iota(I32, (64, LANES), 0)
    lane64 = lax.broadcasted_iota(I32, (64, 64), 1)
    sub64 = lax.broadcasted_iota(I32, (64, 64), 0)
    slot_col = jnp.sum(
        jnp.where(lane64 == sub64, jnp.broadcast_to(slot_row, (64, 64)), 0), axis=1, keepdims=True
    )
    hit = (slot_col >= lane * NBE) & (slot_col < lane * NBE + NBE)
    row_buf[0:1, :] = jnp.sum(jnp.where(hit, sub, 0), axis=0, keepdims=True)
    ids_row = jnp.sum(jnp.where(hit, slot_col + 1, 0), axis=0, keepdims=True) - 1
    tbl = pltpu.make_async_copy(row_buf.at[pl.ds(0, 1)], slot_tbl, tbl_sem.at[0])
    tbl.start()
    ids_line[z] = ids_row

    pl.semaphore_wait(barrier, len(greeted))
    for p in plane:
        pl.semaphore_signal(lines_in, inc=1, device_id=place(*p), device_id_type=MESH)
    loads[0].wait()
    tbl.wait()

    def pack_to(to):
        send[to] = llm[jnp.clip(slot_tbl[0, to], 0, 63)]

    def pack(i):
        s_at, z_at, y_at = partner(i)
        pack_to(s_at * (NZ * NY) + z_at * NY + y_at)

    for i in range(FIRST):
        pack(i)
    pl.semaphore_wait(lines_in, len(plane))

    def spread(partners, source, target_of, s_sem, r_sem):
        for i, p in enumerate(partners):
            pltpu.make_async_remote_copy(
                source, target_of(i), s_sem, r_sem, device_id=place(*p), device_id_type=MESH
            ).start()

    def wait_bytes(ref, sem):
        pltpu.make_async_copy(ref, ref, sem).wait()

    before = wrap(me + SHARDS - 1, SHARDS)
    after = wrap(me + 1, SHARDS)

    def edges(buf, rows, k):
        for j, (to, start, end) in enumerate(
            ((after, FRAMES, 0), (before, rows, rows + FRAMES))
        ):
            pltpu.make_async_remote_copy(
                buf.at[pl.ds(start, rows)],
                buf.at[pl.ds(end, rows)],
                halo_send.at[k, j],
                halo_recv.at[k, j],
                device_id={"sec": to // (NZ * NY), "tm": lax.rem(to, NZ * NY), "dp": dp},
                device_id_type=MESH,
            ).start()

    def edges_in(buf, rows, k):
        wait_bytes(buf.at[pl.ds(0, rows)], halo_recv.at[k, 0])
        wait_bytes(buf.at[pl.ds(0, rows)], halo_recv.at[k, 1])

    def edges_out(buf, rows, k):
        wait_bytes(buf.at[pl.ds(0, rows)], halo_send.at[k, 0])
        wait_bytes(buf.at[pl.ds(0, rows)], halo_send.at[k, 1])

    loads[1].wait()
    edges(enc, EDGE, 0)
    spread(line, ids_line.at[z], lambda i: ids_line.at[z], ids_send.at[0], ids_recv.at[0])

    def block_copy(i):
        s_at, z_at, y_at = partner(i)
        to = s_at * (NZ * NY) + z_at * NY + y_at
        return pltpu.make_async_remote_copy(
            send.at[to],
            recv.at[me],
            a2a_send.at[i],
            a2a_recv,
            device_id=place(s_at, z_at, y_at, dp),
            device_id_type=MESH,
        )

    started = [0]
    ended = [0]

    def begin(count):
        low, high = started[0], min(SENDS, started[0] + count)
        started[0] = high

        def step(i, carry):
            block_copy(i).start()
            return carry

        if high > low:
            lax.fori_loop(low, high, step, 0)

    def settle(left):
        low, high = ended[0], max(ended[0], started[0] - left)
        ended[0] = high

        def step(i, carry):
            block_copy(i).wait_send()
            return carry

        if high > low:
            lax.fori_loop(low, high, step, 0)

    def reserve(count):
        first = started[0]
        started[0] += count
        assert started[0] <= SENDS
        return first

    def pump(first, i):
        block_copy(first + i).start()

    begin(FIRST)

    def pack_more(i, carry):
        for j in range(3):
            pack(FIRST + 3 * i + j)
        return carry

    lax.fori_loop(0, (SENDS - FIRST) // 3, pack_more, 0)
    recv[me] = llm[jnp.clip(slot_tbl[0, me], 0, 63)]
    begin(10)

    gain = small[9:10, :]
    bias = small[10:11, :]

    def norm_rows(values):
        values = values.astype(F32)
        mean = jnp.mean(values, axis=1, keepdims=True)
        centred = values - mean
        scale = lax.rsqrt(jnp.mean(centred * centred, axis=1, keepdims=True) + EPS)
        hat = centred * scale
        return hat, scale, (hat * gain + bias).astype(BF16)

    def norm(r, carry):
        rows = pl.ds(pl.multiple_of(r * 64, 64), 64)
        wide_rows = pl.ds(pl.multiple_of(r * 64 + EDGE, EDGE), 64)
        hat, scale, out = norm_rows(enc[wide_rows, :])
        rstd[rows, :] = jnp.broadcast_to(scale, (64, LANES))
        x_hat[rows, :] = hat
        normed[wide_rows, :] = out
        return carry

    lax.fori_loop(0, 8, norm, 0)

    lengths = jnp.broadcast_to(ints[:, 0:UTT_PAD].astype(F32), (8, UTT_PAD)).astype(BF16)
    upper = (
        lax.broadcasted_iota(I32, (UTT_PAD, UTT_PAD), 0)
        <= lax.broadcasted_iota(I32, (UTT_PAD, UTT_PAD), 1)
    ).astype(F32).astype(BF16)
    ends = jnp.dot(lengths, upper, preferred_element_type=F32)[0:1, :]

    def number(r, carry):
        rows = pl.ds(pl.multiple_of(r * 136, 8), 136)
        position = lax.broadcasted_iota(I32, (136, 1), 0) + (r * 136 + me * FRAMES - EDGE)
        position_f = position.astype(F32)
        count = jnp.sum((position_f >= ends).astype(F32), axis=1, keepdims=True)
        inside = (position >= 0) & (position < SHARDS * FRAMES)
        seg[rows, :] = jnp.broadcast_to(jnp.where(inside, count, -1.0), (136, LANES))
        return carry

    lax.fori_loop(0, WIDE // 136, number, 0)

    def mark(r, carry):
        window = seg[pl.ds(pl.multiple_of(r * THIRD, 16), THIRD + 2 * PAD), :]
        own = window[PAD : PAD + THIRD]
        rows = pl.ds(pl.multiple_of(r * THIRD, 16), THIRD)
        for j in range(TAPS):
            masks[j, rows, :] = (window[HALF + j : HALF + j + THIRD] == own).astype(F32)
        return carry

    lax.fori_loop(0, EXT // THIRD, mark, 0)

    edges_in(enc, EDGE, 0)
    for start in (0, EDGE + FRAMES):
        normed[start : start + EDGE, :] = norm_rows(enc[start : start + EDGE, :])[2]

    loads[2].wait()
    moved = reserve(4)

    def project(n, carry):
        at = pl.ds(pl.multiple_of(n * 256, 256), 256)
        gate_at = pl.ds(pl.multiple_of(C + n * 256, 256), 256)
        lin = jnp.dot(normed[...], w_in[:, at], preferred_element_type=F32)
        gate = jnp.dot(normed[...], w_in[:, gate_at], preferred_element_type=F32)
        pump(moved, n)
        s = jax.nn.sigmoid(gate)
        mixed = lin * s
        sig[:, at] = s[EDGE : EDGE + FRAMES]
        dsig[:, at] = (mixed * (1.0 - s))[EDGE : EDGE + FRAMES]
        gated[:, at] = mixed.astype(BF16).astype(F32)
        return carry

    lax.fori_loop(0, 4, project, 0)

    moved_conv = reserve(4)

    def convolve(c, carry):
        cols = pl.ds(pl.multiple_of(c * LANES, LANES), LANES)
        taps = small[0:TAPS, cols]
        first_sum = jnp.zeros((1, LANES), F32)
        second_sum = jnp.zeros((1, LANES), F32)
        for r in range(EXT // THIRD):
            window = gated[r * THIRD : r * THIRD + THIRD + 2 * PAD, cols]
            total = jnp.zeros((THIRD, LANES), F32)
            for k in range(TAPS):
                part = window[HALF + k : HALF + k + THIRD]
                if k != HALF:
                    part = part * masks[k, r * THIRD : r * THIRD + THIRD, :]
                total = total + taps[k : k + 1, :] * part
            conv[r * THIRD : r * THIRD + THIRD, cols] = total
            own = total[(PAD if r == 0 else 0) : (THIRD - PAD if r == EXT // THIRD - 1 else THIRD)]
            first_sum = first_sum + jnp.sum(own, axis=0, keepdims=True)
            second_sum = second_sum + jnp.sum(own * own, axis=0, keepdims=True)
        ar_src[0, 0, 0, pl.ds(c, 1), :] = first_sum
        ar_src[0, 0, 1, pl.ds(c, 1), :] = second_sum

        @pl.when(lax.rem(c, 2) == 0)
        def _():
            pump(moved_conv, c // 2)

        return carry

    lax.fori_loop(0, COLS, convolve, 0)

    groups = ((mate, ar_s), (cross, ar_xy), (line, ar_z))

    def sum_send(k, step):
        partners, target = groups[step]
        spread(
            partners,
            ar_src.at[k, step],
            lambda i: target.at[k, i],
            ar_send.at[k, step],
            ar_recv.at[k, step],
        )

    def sum_recv(k, step):
        partners, target = groups[step]
        count = len(partners)
        wait_bytes(target.at[k, pl.ds(0, count)], ar_recv.at[k, step])
        total = ar_src[k, step]
        for i in range(count):
            total = total + target[k, i]
        ar_src[k, step + 1] = total

    def sum_done(k):
        for step, (partners, target) in enumerate(groups):
            wait_bytes(target.at[k, pl.ds(0, len(partners))], ar_send.at[k, step])

    sum_send(0, 0)
    begin(4)

    wait_bytes(ids_line.at[pl.ds(0, NZ - 1)], ids_recv.at[0])
    for j in range(NZ):
        ids_tile[j : j + 1, :] = ids_line[j]
    here = sec * NY + y
    ids_all[here] = ids_tile[...]
    spread(plane, ids_tile, lambda i: ids_all.at[here], ids_send.at[1], ids_recv.at[1])

    sum_recv(0, 0)
    sum_send(0, 1)
    begin(14)
    sum_recv(0, 1)
    sum_send(0, 2)
    begin(SENDS)
    sum_recv(0, 2)

    wait_bytes(ids_all.at[pl.ds(0, 7)], ids_recv.at[1])
    ids = ids_all[...].reshape(64, LANES)
    mine = jnp.sum(jnp.where(lane == me, ids, 0), axis=1, keepdims=True) - me * NBE
    quarter = sub // NZ
    source = (quarter // NY) * (NZ * NY) + lax.rem(sub, NZ) * NY + lax.rem(quarter, NY)
    row_buf[1:2, :] = jnp.sum(jnp.where(mine == lane, source, 0), axis=0, keepdims=True)
    src_copy = pltpu.make_async_copy(row_buf.at[pl.ds(1, 1)], src_tbl, tbl_sem.at[1])
    src_copy.start()


    def bn_scales(c):
        bn_mean = ar_src[0, 3, 0, pl.ds(c, 1), :] / ALL_FRAMES
        bn_var = ar_src[0, 3, 1, pl.ds(c, 1), :] / ALL_FRAMES - bn_mean * bn_mean
        return bn_mean, lax.rsqrt(bn_var + EPS)

    def normalise(c, carry):
        cols = pl.ds(pl.multiple_of(c * LANES, LANES), LANES)
        bn_mean, bn_rstd = bn_scales(c)
        bn_gain = small[11:12, cols]
        bn_bias = small[12:13, cols]
        taps = small[0:TAPS, cols]
        factor = bn_gain * bn_rstd
        for r in range(EXT // 48):
            rows = slice(r * 48, r * 48 + 48)
            conv[rows, cols] = (conv[rows, cols] - bn_mean) * bn_rstd
        for r in range(FRAMES // ROWS):
            rows = slice(r * ROWS, r * ROWS + ROWS)
            window = conv[r * ROWS : r * ROWS + ROWS + 2 * PAD, cols]
            pre = window[PAD : PAD + ROWS] * bn_gain + bn_bias
            s = jax.nn.sigmoid(pre)
            swish[rows, cols] = s * (1.0 + pre * (1.0 - s))
            ones_total = jnp.zeros((ROWS, LANES), F32)
            z_total = jnp.zeros((ROWS, LANES), F32)
            for j in range(TAPS):
                weight = (taps[TAPS - 1 - j : TAPS - j, :] * factor) * masks[j, PAD + r * ROWS : PAD + r * ROWS + ROWS, :]
                ones_total = ones_total + weight
                z_total = z_total + weight * window[HALF + j : HALF + j + ROWS]
            ones_t[rows, cols] = ones_total
            z_t[rows, cols] = z_total
        return carry

    lax.fori_loop(0, COLS, normalise, 0)
    src_copy.wait()
    loads[3].wait()
    assert started[0] == SENDS

    settle(8)

    wait_bytes(recv.at[pl.ds(0, SENDS)], a2a_recv)

    def gather(b, carry):
        inc[pl.ds(pl.multiple_of(b * BLK, BLK), BLK), :] = recv[jnp.clip(src_tbl[0, b], 0, 63)]
        return carry

    lax.fori_loop(0, NBE, gather, 0)

    for n in range(4):
        at = slice(n * 256, n * 256 + 256)
        grad = lax.dot_general(inc[...], w_out[at, :], NT, preferred_element_type=F32)
        grad = grad * swish[:, at]
        d_pre[PAD : PAD + FRAMES, at] = grad
        first_sum = jnp.sum(grad, axis=0, keepdims=True)
        cross_sum = jnp.sum(grad * conv[PAD : PAD + FRAMES, at], axis=0, keepdims=True)
        for j in range(2):
            c = 2 * n + j
            ar_src[1, 0, 0, c : c + 1, :] = first_sum[:, j * LANES : (j + 1) * LANES]
            ar_src[1, 0, 1, c : c + 1, :] = cross_sum[:, j * LANES : (j + 1) * LANES]

    def conv_back(c, carry):
        cols = pl.ds(pl.multiple_of(c * LANES, LANES), LANES)
        bn_mean, bn_rstd = bn_scales(c)
        factor = small[11:12, cols] * bn_rstd
        taps = small[0:TAPS, cols] * factor
        for r in range(FRAMES // ROWS):
            rows = slice(r * ROWS, r * ROWS + ROWS)
            window = d_pre[r * ROWS : r * ROWS + ROWS + 2 * PAD, cols]
            total = jnp.zeros((ROWS, LANES), F32)
            for j in range(TAPS):
                part = window[HALF + j : HALF + j + ROWS]
                if j != HALF:
                    part = part * masks[j, PAD + r * ROWS : PAD + r * ROWS + ROWS, :]
                total = total + taps[TAPS - 1 - j : TAPS - j, :] * part
            d_t[rows, cols] = total
        return carry

    sum_send(1, 0)
    edges(d_pre, PAD, 1)
    sum_recv(1, 0)
    sum_send(1, 1)
    edges_in(d_pre, PAD, 1)
    lax.fori_loop(0, COLS // 2, conv_back, 0)
    settle(0)
    wait_bytes(ids_line.at[pl.ds(0, NZ - 1)], ids_send.at[0])
    wait_bytes(ids_all.at[pl.ds(0, 7)], ids_send.at[1])
    edges_out(enc, EDGE, 0)
    sum_done(0)
    sum_recv(1, 1)
    sum_send(1, 2)
    lax.fori_loop(COLS // 2, COLS, conv_back, 0)
    sum_recv(1, 2)

    def assemble(c, carry):
        cols = pl.ds(pl.multiple_of(c * LANES, LANES), LANES)
        gate_cols = pl.ds(pl.multiple_of(C + c * LANES, LANES), LANES)
        grad_mean = ar_src[1, 3, 0, pl.ds(c, 1), :] / ALL_FRAMES
        cross_mean = ar_src[1, 3, 1, pl.ds(c, 1), :] / ALL_FRAMES
        for r in range(FRAMES // ROWS):
            rows = slice(r * ROWS, r * ROWS + ROWS)
            grad = d_t[rows, cols] - grad_mean * ones_t[rows, cols] - cross_mean * z_t[rows, cols]
            d_mixed[rows, cols] = (grad * sig[rows, cols]).astype(BF16)
            d_mixed[rows, gate_cols] = (grad * dsig[rows, cols]).astype(BF16)
        return carry

    lax.fori_loop(0, COLS, assemble, 0)

    for m in range(2):
        part = slice(m * 256, m * 256 + 256)
        h = lax.dot_general(d_mixed[part, :], w_in[...], NT, preferred_element_type=F32) * gain
        hat = x_hat[part, :]
        mean = jnp.mean(h, axis=1, keepdims=True)
        along = jnp.mean(h * hat, axis=1, keepdims=True)
        scale = rstd[part, 0:1]
        out_ref[part, :] = (inc[part, :].astype(F32) + scale * (h - mean - hat * along)).astype(BF16)

    edges_out(d_pre, PAD, 1)
    sum_done(1)


def local(
    enc_input,
    llm_grads,
    slot_block,
    utt_lengths,
    ln_gain,
    ln_bias,
    w_in,
    dw_kernel,
    bn_gain,
    bn_bias,
    w_out,
):
    vmem = pl.BlockSpec(memory_space=pltpu.VMEM)
    hbm = pl.BlockSpec(memory_space=pl.ANY)
    dma = pltpu.SemaphoreType.DMA
    full = pltpu.VMEM((FRAMES, C), F32)
    wide = pltpu.VMEM((EXT, C), F32)
    blocks = pltpu.VMEM((SHARDS, BLK, C), BF16)
    def row(values, at):
        values = values.reshape(-1, C)
        return jnp.pad(values, ((at, SMALL - at - values.shape[0]), (0, 0)))

    small = row(dw_kernel, 0)
    for at, values in enumerate((ln_gain, ln_bias, bn_gain, bn_bias), TAPS):
        small = small + row(values, at)
    ints = jnp.concatenate(
        [jnp.pad(utt_lengths, ((0, 0), (0, UTT_PAD - UTT))), jnp.pad(slot_block, ((0, 0), (0, 64)))], axis=1
    )
    out = pl.pallas_call(
        kernel,
        out_shape=jax.ShapeDtypeStruct((FRAMES, C), BF16),
        in_specs=[hbm] * 4 + [vmem] * 2,
        out_specs=vmem,
        scratch_shapes=[
            pltpu.VMEM((WIDE, C), BF16),
            blocks,
            pltpu.VMEM((C, 2 * C), BF16),
            pltpu.VMEM((C, C), BF16),
            blocks,
            blocks,
            pltpu.VMEM((8, LANES), I32),
            pltpu.SMEM((1, LANES), I32),
            pltpu.SMEM((1, LANES), I32),
            pltpu.VMEM((NZ, 1, LANES), I32),
            pltpu.VMEM((NZ, LANES), I32),
            pltpu.VMEM((8, NZ, LANES), I32),
            pltpu.VMEM((WIDE, LANES), F32),
            pltpu.VMEM((TAPS, EXT, LANES), F32),
            full,
            pltpu.VMEM((FRAMES, LANES), F32),
            pltpu.VMEM((WIDE, C), BF16),
            full,
            full,
            pltpu.VMEM((WIDE, C), F32),
            wide,
            full,
            full,
            full,
            full,
            wide,
            pltpu.VMEM((FRAMES, C), BF16),
            pltpu.VMEM((FRAMES, 2 * C), BF16),
            pltpu.VMEM((2, 4, 2, COLS, LANES), F32),
            pltpu.VMEM((2, 1, 2, COLS, LANES), F32),
            pltpu.VMEM((2, 15, 2, COLS, LANES), F32),
            pltpu.VMEM((2, 7, 2, COLS, LANES), F32),
            dma((4,)),
            dma((2,)),
            dma((SENDS,)),
            dma,
            dma((2,)),
            dma((2,)),
            dma((2, 2)),
            dma((2, 2)),
            dma((2, 3)),
            dma((2, 3)),
            pltpu.SemaphoreType.REGULAR,
        ],
        compiler_params=pltpu.CompilerParams(
            collective_id=1, has_side_effects=True, vmem_limit_bytes=52 << 20
        ),
        name="conv_module_back",
    )(
        enc_input[0],
        llm_grads[0].reshape(SHARDS, BLK, C),
        w_in,
        w_out,
        small,
        ints,
    )
    return out[None]


def solution(mesh):
    in_specs = (
        P("dp", ("sec", "tm"), None),
        P("dp", ("sec", "tm"), None),
        P("dp", ("sec", "tm")),
        P("dp", None),
        P(),
        P(),
        P(),
        P(),
        P(),
        P(),
        P(),
    )
    out_specs = P("dp", ("sec", "tm"), None)
    return jax.shard_map(local, mesh=mesh, in_specs=in_specs, out_specs=out_specs, check_vma=False)
```
